256 devices in a mesh: tm: 32 (over x_hi, z, core), space: 8 (over x_lo, y).
Axes of the slice: x: 4 (x_hi: 2, x_lo: 2; x = x_hi * 2 + x_lo), y: 4, z: 8, core: 2. Of those that a mesh axis runs over, the one named last changes fastest.
Arguments:
- iterate: float32 [32, 1024, 1024], P('tm', 'space'), may hold values from -6 to 6
- forcing: float32 [32, 1024, 1024], P('tm', 'space'), may hold values from -6 to 6
- initial: float32 [1024, 1024], P('space'), may hold values from -6 to 6
- levels: int32 [1024, 1024], P('space'), may hold values from 0 to 7
Outputs:
- increment: float32 [32, 1024, 1024], P('tm', 'space')
The draws below stay inside these ranges and needn't reach their ends.
All inputs are finite; a program needn't handle non-finite values.
Results may differ from the reference program's by a relative error of at most 0.0003.
Values sent between devices are 32-bit elements; how exact they have to be, the bound alone decides.
No kernel may reach another device: no remote copies, remote signals or barrier semaphores. Data moves between devices by JAX's collectives and lax.ppermute only.
A program may use at most 64 MiB of HBM per device.

```python
import math
import jax
import jax.numpy as jnp
from jax import lax

GRID = 1024
STEPS = 32


def touch_ends(array, own_key, low, high):
    extent = array.shape
    spot = [jax.random.randint(jax.random.fold_in(own_key, axis), (), 0, extent[axis]) for axis in range(len(extent))]
    array = array.at[tuple(spot)].set(low)
    longest = extent.index(max(extent))
    spot[longest] = (spot[longest] + 1) % extent[longest]
    return array.at[tuple(spot)].set(high)


def block_levels(rng, extent, cuts, low, high):
    factor_of, own = 1.0, jax.random.fold_in(rng, 6)
    for dim, parts in cuts:
        draws = jnp.exp(jax.random.uniform(jax.random.fold_in(own, dim), (parts,), jnp.float32, low / len(cuts), high / len(cuts)))
        factor_of = factor_of * jnp.repeat(draws, extent[dim] // parts).reshape([-1 if axis == dim else 1 for axis in range(len(extent))])
    return factor_of


def centred(rng, dims, spread, bound, pieces=(), kind=jnp.bfloat16):
    entries = spread * jax.random.normal(rng, dims, jnp.float32)
    if pieces:
        entries = entries * block_levels(rng, dims, pieces, -0.22, 0.18)
    return jnp.clip(entries, -bound, bound).astype(kind)


def setup_inputs(seed: int = 0) -> dict:
    seeds = jax.random.split(jax.random.key(seed), 5)
    return {
        "iterate": centred(seeds[0], (STEPS, GRID, GRID), 1.0, 6.0, ((0, 32), (1, 8)), jnp.float32),
        "forcing": centred(seeds[1], (STEPS, GRID, GRID), 1.0, 6.0, ((0, 32), (1, 8)), jnp.float32),
        "initial": centred(seeds[2], (GRID, GRID), 1.0, 6.0, ((0, 8),), jnp.float32),
        "levels": touch_ends(jax.random.randint(seeds[3], (GRID, GRID), 0, 8), jax.random.fold_in(seeds[3], 1), 0, 7).astype(jnp.int32),
    }


TIME_STEP = 0.05
CIRCULANT_ALPHA = 0.1
MEAN_DAMPING = 5.25
DAMPING_TABLE = (0.5, 1.0, 1.5, 2.5, 4.0, 6.0, 8.0, 10.0)


def laplacian(field):
    return (jnp.roll(field, 1, -2) + jnp.roll(field, -1, -2) + jnp.roll(field, 1, -1)
            + jnp.roll(field, -1, -1) - 4.0 * field)


def reference(iterate, forcing, initial, levels):
    table = jnp.asarray(DAMPING_TABLE, jnp.float32)
    damping = jnp.take(table, levels, axis=0)
    previous = jnp.concatenate([initial[None], iterate[:-1]], axis=0)
    lap_one = laplacian(iterate)
    operator = lap_one + laplacian(lap_one) + damping[None] * iterate
    grad_rows = 0.5 * (jnp.roll(iterate, -1, -2) - jnp.roll(iterate, 1, -2))
    grad_cols = 0.5 * (jnp.roll(iterate, -1, -1) - jnp.roll(iterate, 1, -1))
    residual = (previous + TIME_STEP * forcing - iterate - TIME_STEP * operator
                - TIME_STEP * 0.5 * (grad_rows * grad_rows + grad_cols * grad_cols))
    positions = jnp.arange(STEPS).astype(residual.dtype)
    weights = jnp.exp(positions * (math.log(CIRCULANT_ALPHA) / STEPS))
    spectra = jnp.fft.fft(residual * weights[:, None, None], axis=0)
    beta = CIRCULANT_ALPHA ** (1.0 / STEPS)
    angles = positions * (2.0 * math.pi / STEPS)
    diag_real = 1.0 - beta * jnp.cos(angles)
    diag_imag = beta * jnp.sin(angles)
    grid_pos = jnp.arange(GRID).astype(residual.dtype)
    sine_sq = 4.0 * jnp.sin(math.pi * grid_pos / GRID) ** 2
    modes = sine_sq[:, None] + sine_sq[None, :]
    spatial = TIME_STEP * (modes * modes - modes + MEAN_DAMPING)
    excess = -TIME_STEP * (damping - MEAN_DAMPING)

    def solve_one(packed):
        spectrum, dreal, dimag = packed
        symbol = (dreal + spatial) + 1j * dimag
        first = jnp.fft.ifft2(jnp.fft.fft2(spectrum) / symbol)
        return first + jnp.fft.ifft2(jnp.fft.fft2(excess * first) / symbol)

    solved = lax.map(solve_one, (spectra, diag_real, diag_imag))
    increment = jnp.fft.ifft(solved, axis=0).real / weights[:, None, None]
    return increment.astype(jnp.float32)
```

```python
import functools
import math

import jax
import jax.numpy as jnp
import ml_dtypes
import numpy as np
from jax import lax
from jax.experimental import pallas as pl
from jax.experimental.pallas import tpu as pltpu
from jax.sharding import PartitionSpec as P

TIME_STEP = 0.05
CIRCULANT_ALPHA = 0.1
MEAN_DAMPING = 5.25
DAMPING_TABLE = (0.5, 1.0, 1.5, 2.5, 4.0, 6.0, 8.0, 10.0)
GROUP = ("space", "tm")
VMEM = pl.BlockSpec(memory_space=pltpu.VMEM)
SMEM = pl.BlockSpec(memory_space=pltpu.SMEM)


def hartley_tables(length):
    positions = np.arange(length, dtype=np.int64)
    angle = (positions[:, None] * positions[None, :] % length) * (2.0 * math.pi / length)
    table = (np.cos(angle) + np.sin(angle)) / math.sqrt(length)
    high = table.astype(ml_dtypes.bfloat16)
    low = (table - high.astype(np.float64)).astype(ml_dtypes.bfloat16)
    return high, low


def pieces(block):
    high = block.astype(jnp.bfloat16)
    low = (block - high.astype(jnp.float32)).astype(jnp.bfloat16)
    return high, low


def product(a, b, dims):
    return lax.dot_general(a, b, (dims, ((), ())), preferred_element_type=jnp.float32)


def from_left(table_high, table_low, block, dims=((1,), (0,))):
    high, low = pieces(block)
    axis = 1 - dims[1][0]
    count = block.shape[axis]
    wide = product(table_high, jnp.concatenate([high, low], axis=axis), dims)
    return wide[:, :count] + wide[:, count:] + product(table_low, high, dims)


def from_right(block, table_high, table_low):
    high, low = pieces(block)
    count = block.shape[0]
    dims = ((1,), (0,))
    tall = product(jnp.concatenate([high, low], axis=0), table_high, dims)
    return tall[:count] + tall[count:] + product(high, table_low, dims)


def excess_of(levels):
    excess = jnp.full(levels.shape, -TIME_STEP * (DAMPING_TABLE[0] - MEAN_DAMPING), jnp.float32)
    for level_id in range(1, len(DAMPING_TABLE)):
        value = -TIME_STEP * (DAMPING_TABLE[level_id] - MEAN_DAMPING)
        excess = jnp.where(levels == level_id, value, excess)
    return excess


def roll(block, amount, axis):
    return pltpu.roll(block, amount % block.shape[axis], axis)


def source_kernel(steps, step_ref, x_ref, above_ref, below_ref, forcing_ref, initial_ref, levels_ref,
                  high_ref, low_ref, out_ref, source_ref):
    x = x_ref[...]
    rows, width = x.shape
    row = lax.broadcasted_iota(jnp.int32, (rows, width), 0)
    above, below = above_ref[...], below_ref[...]

    def neighbours(block, before, after):
        up = jnp.where(row == 0, before, roll(block, 1, 0))
        down = jnp.where(row == rows - 1, after, roll(block, -1, 0))
        return up, down, roll(block, 1, 1), roll(block, -1, 1)

    def sides(line):
        return roll(line, 1, 1) + roll(line, -1, 1)

    up, down, left, right = neighbours(x, above[1:2], below[0:1])
    grad_rows, grad_cols = down - up, right - left
    source_ref[...] = (
        excess_of(levels_ref[...]) * x
        + TIME_STEP * forcing_ref[...]
        - (TIME_STEP / 8.0) * (grad_rows * grad_rows + grad_cols * grad_cols)
    )

    @pl.when(step_ref[0] == 0)
    def _():
        source_ref[...] += initial_ref[...]

    @pl.when(step_ref[0] == steps - 1)
    def _():
        lap = up + down + left + right - 4.0 * x
        lap_above = above[0:1] + x[0:1] + sides(above)[1:2] - 4.0 * above[1:2]
        lap_below = x[rows - 1 : rows] + below[1:2] + sides(below)[0:1] - 4.0 * below[0:1]
        up2, down2, left2, right2 = neighbours(lap, lap_above, lap_below)
        lap_two = up2 + down2 + left2 + right2 - 4.0 * lap
        source_ref[...] -= x + TIME_STEP * (lap + lap_two + MEAN_DAMPING * x)

    out_ref[...] = from_left(high_ref[...], low_ref[...], source_ref[...], ((1,), (1,)))


def turned_kernel(steps, step_ref, x_ref, levels_ref, x_out, excess_out):
    keep = jnp.where(step_ref[0] == steps - 1, 0.0, 1.0)
    x_out[...] = (x_ref[...] * keep).T
    excess_out[...] = excess_of(levels_ref[...]).T


def solve_kernel(slabs, steps, x_ref, gain_ref, high_ref, low_ref, out_ref):
    rows = x_ref.shape[0] // slabs
    high, low = high_ref[...], low_ref[...]
    fields = jnp.concatenate([x_ref[pl.ds(s * rows, rows), :] for s in range(slabs)], axis=1)
    spectrum = from_right(fields, high, low)
    width = spectrum.shape[1]
    gain = gain_ref[...]
    comps = rows // steps
    pack = gain.shape[0]
    powers = [gain]
    while len(powers) < steps.bit_length():
        powers.append(powers[-1] * powers[-1])
    start = gain / (1.0 - CIRCULANT_ALPHA * powers[-1])
    groups = rows // pack
    u = spectrum.reshape(groups, pack, width) * start[None]
    lane_row = lax.broadcasted_iota(jnp.int32, (1, pack, width), 1)
    for j in range(steps.bit_length() - 1):
        shift = comps << j
        if shift < pack:
            moved = roll(u.reshape(rows, width), shift, 0).reshape(u.shape)
            head = jnp.where(lane_row < shift, CIRCULANT_ALPHA * moved[:1], moved[:1])
            moved = jnp.concatenate([head, moved[1:]], axis=0)
        else:
            k = shift // pack
            moved = jnp.concatenate([CIRCULANT_ALPHA * u[groups - k :], u[: groups - k]], axis=0)
        u = u + powers[j][None] * moved
    result = from_right(u.reshape(rows, width), high, low)
    for s in range(slabs):
        out_ref[pl.ds(s * rows, rows), :] = result[:, s * rows : (s + 1) * rows]


def sweep_kernel(y_ref, x_ref, excess_ref, high_ref, low_ref, out_ref, first_ref):
    high, low = high_ref[...], low_ref[...]
    first = from_left(high, low, y_ref[...]) - x_ref[...]
    first_ref[...] = first
    out_ref[...] = from_left(high, low, excess_ref[...] * first)


def finish_kernel(y_ref, first_ref, high_ref, low_ref, out_ref):
    out_ref[...] = (from_left(high_ref[...], low_ref[...], y_ref[...]) + first_ref[...]).T


def call(kernel, out_shapes, specs, scratch=(), flops=0, bytes_accessed=0):
    return pl.pallas_call(
        kernel,
        out_shape=out_shapes,
        in_specs=specs,
        out_specs=[VMEM] * len(out_shapes) if isinstance(out_shapes, (list, tuple)) else VMEM,
        scratch_shapes=list(scratch),
        compiler_params=pltpu.CompilerParams(vmem_limit_bytes=48 * 1024 * 1024),
        cost_estimate=pl.CostEstimate(flops=flops, bytes_accessed=bytes_accessed, transcendentals=0),
    )


def local(iterate, forcing, initial, levels):
    field = iterate[0]
    rows, width = field.shape
    steps, slabs = lax.axis_size("tm"), lax.axis_size("space")
    devices = steps * slabs
    comps = width // devices
    high, low = (jnp.asarray(t) for t in hartley_tables(width))
    step = lax.axis_index("tm").astype(jnp.int32).reshape(1)
    turned = jax.ShapeDtypeStruct((width, rows), jnp.float32)
    work = 6 * rows * width * width
    moved_bytes = 4 * width * width + 16 * rows * width

    ahead = [(i, (i + 1) % slabs) for i in range(slabs)]
    above = lax.ppermute(field[rows - 2 :], "space", ahead)
    below = lax.ppermute(field[:2], "space", [(j, i) for i, j in ahead])

    def exchange(block):
        return lax.all_to_all(
            block.reshape(devices, comps, rows), GROUP, split_axis=0, concat_axis=0, tiled=True
        ).reshape(width, rows)

    def waves(index):
        return 4.0 * jnp.sin(math.pi * index.astype(jnp.float32) / width) ** 2

    mine = lax.axis_index("space") * steps + lax.axis_index("tm")
    column = mine * comps + jnp.arange(8, dtype=jnp.int32) % comps
    modes = waves(column)[:, None] + waves(jnp.arange(width, dtype=jnp.int32))[None, :]
    gain = 1.0 / (1.0 + TIME_STEP * (modes * modes - modes + MEAN_DAMPING))

    sent = call(
        functools.partial(source_kernel, steps), turned, [SMEM] + [VMEM] * 8,
        scratch=[pltpu.VMEM((rows, width), jnp.float32)], flops=work, bytes_accessed=moved_bytes,
    )(step, field, above, below, forcing[0], initial, levels, high, low)
    kept, excess = call(
        functools.partial(turned_kernel, steps), [turned, turned], [SMEM, VMEM, VMEM],
        flops=16 * rows * width, bytes_accessed=16 * rows * width,
    )(step, field, levels)

    solve = call(
        functools.partial(solve_kernel, slabs, steps), turned, [VMEM] * 4,
        flops=2 * work, bytes_accessed=moved_bytes,
    )
    back = exchange(solve(exchange(sent), gain, high, low))
    error, first = call(
        sweep_kernel, [turned, turned], [VMEM] * 5, flops=2 * work, bytes_accessed=moved_bytes
    )(back, kept, excess, high, low)
    last = exchange(solve(exchange(error), gain, high, low))
    increment = call(
        finish_kernel, jax.ShapeDtypeStruct((rows, width), jnp.float32), [VMEM] * 4,
        flops=work, bytes_accessed=moved_bytes,
    )(last, first, high, low)
    return increment[None]


def solution(mesh):
    placed = (P("tm", "space", None), P("tm", "space", None), P("space", None), P("space", None))
    return jax.shard_map(
        local, mesh=mesh, in_specs=placed, out_specs=P("tm", "space", None), check_vma=False
    )
```

```python
import functools
import math

import jax
import jax.numpy as jnp
import ml_dtypes
import numpy as np
from jax import lax
from jax.experimental import pallas as pl
from jax.experimental.pallas import tpu as pltpu
from jax.sharding import PartitionSpec as P

TIME_STEP = 0.05
CIRCULANT_ALPHA = 0.1
MEAN_DAMPING = 5.25
DAMPING_TABLE = (0.5, 1.0, 1.5, 2.5, 4.0, 6.0, 8.0, 10.0)
AXES = {"xh": 2, "z": 8, "c": 2, "xl": 2, "y": 4}
TIME = ("xh", "z", "c")
SLAB = ("xl", "y")
GROUP = ("xl", "y", "z", "c", "xh")
VMEM = pl.BlockSpec(memory_space=pltpu.VMEM)
SMEM = pl.BlockSpec(memory_space=pltpu.SMEM)
HBM = pl.BlockSpec(memory_space=pltpu.HBM)


def hartley_tables(length):
    positions = np.arange(length, dtype=np.int64)
    angle = (positions[:, None] * positions[None, :] % length) * (2.0 * math.pi / length)
    table = (np.cos(angle) + np.sin(angle)) / math.sqrt(length)
    high = table.astype(ml_dtypes.bfloat16)
    low = (table - high.astype(np.float64)).astype(ml_dtypes.bfloat16)
    return high, low


def pieces(block):
    high = block.astype(jnp.bfloat16)
    low = (block - high.astype(jnp.float32)).astype(jnp.bfloat16)
    return high, low


def product(a, b, dims):
    return lax.dot_general(a, b, (dims, ((), ())), preferred_element_type=jnp.float32)


def from_right(block, table_high, table_low):
    high, low = pieces(block)
    count = block.shape[0]
    dims = ((1,), (0,))
    tall = product(jnp.concatenate([high, low], axis=0), table_high, dims)
    return tall[:count] + tall[count:] + product(high, table_low, dims)


def excess_of(levels):
    excess = jnp.full(levels.shape, -TIME_STEP * (DAMPING_TABLE[0] - MEAN_DAMPING), jnp.float32)
    for level_id in range(1, len(DAMPING_TABLE)):
        value = -TIME_STEP * (DAMPING_TABLE[level_id] - MEAN_DAMPING)
        excess = jnp.where(levels == level_id, value, excess)
    return excess


def roll(block, amount, axis):
    return pltpu.roll(block, amount % block.shape[axis], axis)


def load_kernel(step_ref, x_hbm, forcing_hbm, initial_hbm, levels_hbm, high_hbm, low_hbm,
                x_ref, base_ref, excess_ref, high_ref, low_ref,
                forcing_ref, initial_ref, levels_ref, sems):
    pairs = [(x_hbm, x_ref), (levels_hbm, levels_ref), (forcing_hbm, forcing_ref),
             (initial_hbm, initial_ref), (high_hbm, high_ref), (low_hbm, low_ref)]
    copies = [pltpu.make_async_copy(a, b, sems.at[i]) for i, (a, b) in enumerate(pairs)]
    for copy in copies:
        copy.start()
    copies[0].wait()
    copies[1].wait()
    x = x_ref[...]
    excess = excess_of(levels_ref[...])
    excess_ref[...] = excess
    grad_cols = roll(x, -1, 1) - roll(x, 1, 1)
    copies[2].wait()
    base_ref[...] = (
        excess * x + TIME_STEP * forcing_ref[...] - (TIME_STEP / 8.0) * (grad_cols * grad_cols)
    )
    copies[3].wait()

    @pl.when(step_ref[0] == 0)
    def _():
        base_ref[...] += initial_ref[...]

    copies[4].wait()
    copies[5].wait()


def source_kernel(steps, step_ref, x_ref, above_ref, below_ref, base_ref, high_ref, low_ref,
                  out_ref, source_ref):
    x = x_ref[...]
    rows, width = x.shape
    row = lax.broadcasted_iota(jnp.int32, (rows, width), 0)
    above, below = above_ref[...], below_ref[...]

    def neighbours(block, before, after):
        up = jnp.where(row == 0, before, roll(block, 1, 0))
        down = jnp.where(row == rows - 1, after, roll(block, -1, 0))
        return up, down

    def sides(line):
        return roll(line, 1, 1) + roll(line, -1, 1)

    up, down = neighbours(x, above[1:2], below[0:1])
    grad_rows = down - up
    source_ref[...] = base_ref[...] - (TIME_STEP / 8.0) * (grad_rows * grad_rows)

    @pl.when(step_ref[0] == steps - 1)
    def _():
        lap = up + down + sides(x) - 4.0 * x
        lap_above = above[0:1] + x[0:1] + sides(above)[1:2] - 4.0 * above[1:2]
        lap_below = x[rows - 1 : rows] + below[1:2] + sides(below)[0:1] - 4.0 * below[0:1]
        up2, down2 = neighbours(lap, lap_above, lap_below)
        lap_two = up2 + down2 + sides(lap) - 4.0 * lap
        source_ref[...] -= x + TIME_STEP * (lap + lap_two + MEAN_DAMPING * x)

    out_ref[...] = from_right(source_ref[...], high_ref[...], low_ref[...]).T


def solve_kernel(slabs, steps, x_ref, gain_ref, high_ref, low_ref, out_ref):
    rows = x_ref.shape[0] // slabs
    high, low = high_ref[...], low_ref[...]
    fields = jnp.concatenate([x_ref[pl.ds(s * rows, rows), :] for s in range(slabs)], axis=1)
    spectrum = from_right(fields, high, low)
    width = spectrum.shape[1]
    gain = gain_ref[...]
    powers = [gain]
    while len(powers) < steps.bit_length():
        powers.append(powers[-1] * powers[-1])
    start = gain / (1.0 - CIRCULANT_ALPHA * powers[-1])
    pack = gain.shape[0]
    half = pack // 2
    groups = rows // pack
    lane_row = lax.broadcasted_iota(jnp.int32, (1, pack, width), 1)
    u = spectrum.reshape(groups, pack, width) * start[None]

    def around(block):
        turned = roll(block.reshape(-1, width), half, 0).reshape(block.shape)
        if block.shape[0] > 1:
            other = roll(block.reshape(-1, width), -half, 0).reshape(block.shape)
            turned = jnp.where(lane_row < half, other, turned)
        return jnp.where(lane_row < half, CIRCULANT_ALPHA, 1.0) * turned

    for j in range(steps.bit_length() - 1):
        k = 1 << j
        if k < groups:
            moved = jnp.concatenate([around(u[groups - k :]), u[: groups - k]], axis=0)
        else:
            moved = around(u)
        u = u + powers[j][None] * moved
    result = from_right(u.reshape(rows, width), high, low)
    for s in range(slabs):
        out_ref[pl.ds(s * rows, rows), :] = result[:, s * rows : (s + 1) * rows]


def sweep_kernel(steps, step_ref, y_ref, x_ref, excess_ref, high_ref, low_ref, out_ref, first_ref):
    high, low = high_ref[...], low_ref[...]
    keep = jnp.where(step_ref[0] == steps - 1, 0.0, 1.0)
    first = from_right(y_ref[...].T, high, low) - keep * x_ref[...]
    first_ref[...] = first
    out_ref[...] = from_right(excess_ref[...] * first, high, low).T


def finish_kernel(y_ref, first_ref, high_ref, low_ref, out_ref):
    out_ref[...] = from_right(y_ref[...].T, high_ref[...], low_ref[...]) + first_ref[...]


def call(kernel, out_shapes, specs, scratch=(), flops=0, bytes_accessed=0):
    return pl.pallas_call(
        kernel,
        out_shape=out_shapes,
        in_specs=specs,
        out_specs=[VMEM] * len(out_shapes) if isinstance(out_shapes, (list, tuple)) else VMEM,
        scratch_shapes=list(scratch),
        compiler_params=pltpu.CompilerParams(vmem_limit_bytes=16 * 1024 * 1024),
        cost_estimate=pl.CostEstimate(flops=flops, bytes_accessed=bytes_accessed, transcendentals=0),
    )


def local(iterate, forcing, initial, levels):
    field = iterate[0]
    rows, width = field.shape
    steps, slabs = lax.axis_size(TIME), lax.axis_size(SLAB)
    devices = steps * slabs
    comps = width // devices
    high, low = (jnp.asarray(t) for t in hartley_tables(width))
    step = lax.axis_index(TIME).astype(jnp.int32).reshape(1)
    plane = jax.ShapeDtypeStruct((rows, width), jnp.float32)
    turned = jax.ShapeDtypeStruct((width, rows), jnp.float32)
    table = jax.ShapeDtypeStruct((width, width), jnp.bfloat16)
    work = 6 * rows * width * width
    moved_bytes = 4 * width * width + 16 * rows * width

    ahead = [(i, (i + 1) % slabs) for i in range(slabs)]
    above = lax.ppermute(field[rows - 2 :], SLAB, ahead)
    below = lax.ppermute(field[:2], SLAB, [(j, i) for i, j in ahead])

    def exchange(block):
        return lax.all_to_all(
            block.reshape(devices, comps, rows), GROUP, split_axis=0, concat_axis=0, tiled=True
        ).reshape(width, rows)

    def waves(index):
        return 4.0 * jnp.sin(math.pi * index.astype(jnp.float32) / width) ** 2

    column = lax.axis_index(GROUP) * comps + jnp.arange(2 * comps, dtype=jnp.int32) % comps
    modes = waves(column)[:, None] + waves(jnp.arange(width, dtype=jnp.int32))[None, :]
    gain = 1.0 / (1.0 + TIME_STEP * (modes * modes - modes + MEAN_DAMPING))

    field, base, excess, high, low = call(
        load_kernel, [plane, plane, plane, table, table], [SMEM] + [HBM] * 6,
        scratch=[pltpu.VMEM((rows, width), jnp.float32), pltpu.VMEM((rows, width), jnp.float32),
                 pltpu.VMEM((rows, width), jnp.int32), pltpu.SemaphoreType.DMA((6,))],
        flops=32 * rows * width, bytes_accessed=moved_bytes,
    )(step, field, forcing[0], initial, levels, high, low)
    sent = call(
        functools.partial(source_kernel, steps), turned, [SMEM] + [VMEM] * 6,
        scratch=[pltpu.VMEM((rows, width), jnp.float32)], flops=work, bytes_accessed=moved_bytes,
    )(step, field, above, below, base, high, low)
    solve = call(
        functools.partial(solve_kernel, slabs, steps), turned, [VMEM] * 4,
        flops=2 * work, bytes_accessed=moved_bytes,
    )
    back = exchange(solve(exchange(sent), gain, high, low))
    error, first = call(
        functools.partial(sweep_kernel, steps), [turned, plane], [SMEM] + [VMEM] * 5,
        flops=2 * work, bytes_accessed=moved_bytes,
    )(step, back, field, excess, high, low)
    last = exchange(solve(exchange(error), gain, high, low))
    increment = call(
        finish_kernel, plane, [VMEM] * 4, flops=work, bytes_accessed=moved_bytes
    )(last, first, high, low)
    return increment[None]


def solution(mesh):
    fine = jax.sharding.Mesh(mesh.devices.reshape(tuple(AXES.values())), tuple(AXES))
    placed = (P(TIME, SLAB, None), P(TIME, SLAB, None), P(SLAB, None), P(SLAB, None))
    return jax.shard_map(
        local, mesh=fine, in_specs=placed, out_specs=P(TIME, SLAB, None), check_vma=False
    )
```

```python
import functools
import math

import jax
import jax.numpy as jnp
import ml_dtypes
import numpy as np
from jax import lax
from jax.experimental import pallas as pl
from jax.experimental.pallas import tpu as pltpu
from jax.sharding import PartitionSpec as P

TIME_STEP = 0.05
CIRCULANT_ALPHA = 0.1
MEAN_DAMPING = 5.25
DAMPING_TABLE = (0.5, 1.0, 1.5, 2.5, 4.0, 6.0, 8.0, 10.0)
AXES = {"xh": 2, "z": 8, "c": 2, "xl": 2, "y": 4}
TIME = ("xh", "z", "c")
SLAB = ("xl", "y")
GROUP = ("xl", "y", "z", "c", "xh")
VMEM = pl.BlockSpec(memory_space=pltpu.VMEM)
SMEM = pl.BlockSpec(memory_space=pltpu.SMEM)
HBM = pl.BlockSpec(memory_space=pltpu.HBM)


def hartley_tables(length):
    positions = np.arange(length, dtype=np.int64)
    angle = (positions[:, None] * positions[None, :] % length) * (2.0 * math.pi / length)
    table = (np.cos(angle) + np.sin(angle)) / math.sqrt(length)
    high = table.astype(ml_dtypes.bfloat16)
    low = (table - high.astype(np.float64)).astype(ml_dtypes.bfloat16)
    return high, low


def pieces(block):
    high = block.astype(jnp.bfloat16)
    low = (block - high.astype(jnp.float32)).astype(jnp.bfloat16)
    return high, low


def product(a, b, dims):
    return lax.dot_general(a, b, (dims, ((), ())), preferred_element_type=jnp.float32)


def from_right(block, table_high, table_low):
    high, low = pieces(block)
    count = block.shape[0]
    dims = ((1,), (0,))
    tall = product(jnp.concatenate([high, low], axis=0), table_high, dims)
    return tall[:count] + tall[count:] + product(high, table_low, dims)


def excess_of(levels):
    excess = jnp.full(levels.shape, -TIME_STEP * (DAMPING_TABLE[0] - MEAN_DAMPING), jnp.float32)
    for level_id in range(1, len(DAMPING_TABLE)):
        value = -TIME_STEP * (DAMPING_TABLE[level_id] - MEAN_DAMPING)
        excess = jnp.where(levels == level_id, value, excess)
    return excess


def roll(block, amount, axis):
    return pltpu.roll(block, amount % block.shape[axis], axis)


def waves(index, width):
    return 4.0 * jnp.sin(index.astype(jnp.float32) * (math.pi / width)) ** 2


def load_kernel(step_ref, column_ref, x_hbm, forcing_hbm, initial_hbm, levels_hbm, high_hbm, low_hbm,
                x_ref, base_ref, excess_ref, high_ref, low_ref, gain_ref,
                forcing_ref, initial_ref, levels_ref, sems):
    pairs = [(x_hbm, x_ref), (levels_hbm, levels_ref), (forcing_hbm, forcing_ref),
             (initial_hbm, initial_ref), (high_hbm, high_ref), (low_hbm, low_ref)]
    copies = [pltpu.make_async_copy(a, b, sems.at[i]) for i, (a, b) in enumerate(pairs)]
    for copy in copies:
        copy.start()
    shape = gain_ref.shape
    comps = shape[0] // 2
    lane = lax.broadcasted_iota(jnp.int32, shape, 1)
    row = lax.broadcasted_iota(jnp.int32, shape, 0)
    column = column_ref[0] + jnp.where(row >= comps, row - comps, row)
    modes = waves(lane, shape[1]) + waves(column, shape[1])
    gain_ref[...] = 1.0 / (1.0 + TIME_STEP * (modes * modes - modes + MEAN_DAMPING))
    copies[0].wait()
    copies[1].wait()
    x = x_ref[...]
    excess = excess_of(levels_ref[...])
    excess_ref[...] = excess
    grad_cols = roll(x, -1, 1) - roll(x, 1, 1)
    copies[2].wait()
    base_ref[...] = (
        excess * x + TIME_STEP * forcing_ref[...] - (TIME_STEP / 8.0) * (grad_cols * grad_cols)
    )
    copies[3].wait()

    @pl.when(step_ref[0] == 0)
    def _():
        base_ref[...] += initial_ref[...]

    copies[4].wait()
    copies[5].wait()


def source_kernel(steps, step_ref, x_ref, above_ref, below_ref, base_ref, high_ref, low_ref,
                  out_ref, source_ref):
    x = x_ref[...]
    rows, width = x.shape
    row = lax.broadcasted_iota(jnp.int32, (rows, width), 0)
    above, below = above_ref[...], below_ref[...]

    def neighbours(block, before, after):
        up = jnp.where(row == 0, before, roll(block, 1, 0))
        down = jnp.where(row == rows - 1, after, roll(block, -1, 0))
        return up, down

    def sides(line):
        return roll(line, 1, 1) + roll(line, -1, 1)

    up, down = neighbours(x, above[1:2], below[0:1])
    grad_rows = down - up
    source_ref[...] = base_ref[...] - (TIME_STEP / 8.0) * (grad_rows * grad_rows)

    @pl.when(step_ref[0] == steps - 1)
    def _():
        lap = up + down + sides(x) - 4.0 * x
        lap_above = above[0:1] + x[0:1] + sides(above)[1:2] - 4.0 * above[1:2]
        lap_below = x[rows - 1 : rows] + below[1:2] + sides(below)[0:1] - 4.0 * below[0:1]
        up2, down2 = neighbours(lap, lap_above, lap_below)
        lap_two = up2 + down2 + sides(lap) - 4.0 * lap
        source_ref[...] -= x + TIME_STEP * (lap + lap_two + MEAN_DAMPING * x)

    out_ref[...] = from_right(source_ref[...], high_ref[...], low_ref[...]).T


def solve_kernel(slabs, steps, x_ref, gain_ref, high_ref, low_ref, out_ref):
    rows = x_ref.shape[0] // slabs
    high, low = high_ref[...], low_ref[...]
    fields = jnp.concatenate([x_ref[pl.ds(s * rows, rows), :] for s in range(slabs)], axis=1)
    spectrum = from_right(fields, high, low)
    width = spectrum.shape[1]
    gain = gain_ref[...]
    powers = [gain]
    while len(powers) < steps.bit_length():
        powers.append(powers[-1] * powers[-1])
    start = gain / (1.0 - CIRCULANT_ALPHA * powers[-1])
    pack = gain.shape[0]
    half = pack // 2
    groups = rows // pack
    lane_row = lax.broadcasted_iota(jnp.int32, (1, pack, width), 1)
    u = spectrum.reshape(groups, pack, width) * start[None]

    def around(block):
        turned = roll(block.reshape(-1, width), half, 0).reshape(block.shape)
        if block.shape[0] > 1:
            other = roll(block.reshape(-1, width), -half, 0).reshape(block.shape)
            turned = jnp.where(lane_row < half, other, turned)
        return jnp.where(lane_row < half, CIRCULANT_ALPHA, 1.0) * turned

    for j in range(steps.bit_length() - 1):
        k = 1 << j
        if k < groups:
            moved = jnp.concatenate([around(u[groups - k :]), u[: groups - k]], axis=0)
        else:
            moved = around(u)
        u = u + powers[j][None] * moved
    result = from_right(u.reshape(rows, width), high, low)
    for s in range(slabs):
        out_ref[pl.ds(s * rows, rows), :] = result[:, s * rows : (s + 1) * rows]


def sweep_kernel(steps, step_ref, y_ref, x_ref, excess_ref, high_ref, low_ref, out_ref, first_ref):
    high, low = high_ref[...], low_ref[...]
    keep = jnp.where(step_ref[0] == steps - 1, 0.0, 1.0)
    first = from_right(y_ref[...].T, high, low) - keep * x_ref[...]
    first_ref[...] = first
    out_ref[...] = from_right(excess_ref[...] * first, high, low).T


def finish_kernel(y_ref, first_ref, high_ref, low_ref, out_ref):
    out_ref[...] = from_right(y_ref[...].T, high_ref[...], low_ref[...]) + first_ref[...]


def call(kernel, out_shapes, specs, scratch=(), flops=0, bytes_accessed=0):
    return pl.pallas_call(
        kernel,
        out_shape=out_shapes,
        in_specs=specs,
        out_specs=[VMEM] * len(out_shapes) if isinstance(out_shapes, (list, tuple)) else VMEM,
        scratch_shapes=list(scratch),
        compiler_params=pltpu.CompilerParams(vmem_limit_bytes=16 * 1024 * 1024),
        cost_estimate=pl.CostEstimate(flops=flops, bytes_accessed=bytes_accessed, transcendentals=0),
    )


def local(iterate, forcing, initial, levels):
    field = iterate[0]
    rows, width = field.shape
    steps, slabs = lax.axis_size(TIME), lax.axis_size(SLAB)
    devices = steps * slabs
    comps = width // devices
    high, low = (jnp.asarray(t) for t in hartley_tables(width))
    step = lax.axis_index(TIME).astype(jnp.int32).reshape(1)
    plane = jax.ShapeDtypeStruct((rows, width), jnp.float32)
    turned = jax.ShapeDtypeStruct((width, rows), jnp.float32)
    table = jax.ShapeDtypeStruct((width, width), jnp.bfloat16)
    work = 6 * rows * width * width
    moved_bytes = 4 * width * width + 16 * rows * width

    ahead = [(i, (i + 1) % slabs) for i in range(slabs)]
    above = lax.ppermute(field[rows - 2 :], SLAB, ahead)
    below = lax.ppermute(field[:2], SLAB, [(j, i) for i, j in ahead])

    def exchange(block):
        return lax.all_to_all(
            block.reshape(devices, comps, rows), GROUP, split_axis=0, concat_axis=0, tiled=True
        ).reshape(width, rows)

    column = (lax.axis_index(GROUP) * comps).astype(jnp.int32).reshape(1)
    gains = jax.ShapeDtypeStruct((2 * comps, width), jnp.float32)
    stay = [pltpu.with_memory_space_constraint(a, pltpu.HBM)
            for a in (field, forcing[0], initial, levels, high, low)]

    field, base, excess, high, low, gain = call(
        load_kernel, [plane, plane, plane, table, table, gains], [SMEM] * 2 + [HBM] * 6,
        scratch=[pltpu.VMEM((rows, width), jnp.float32), pltpu.VMEM((rows, width), jnp.float32),
                 pltpu.VMEM((rows, width), jnp.int32), pltpu.SemaphoreType.DMA((6,))],
        flops=32 * rows * width, bytes_accessed=moved_bytes,
    )(step, column, *stay)
    sent = call(
        functools.partial(source_kernel, steps), turned, [SMEM] + [VMEM] * 6,
        scratch=[pltpu.VMEM((rows, width), jnp.float32)], flops=work, bytes_accessed=moved_bytes,
    )(step, field, above, below, base, high, low)
    solve = call(
        functools.partial(solve_kernel, slabs, steps), turned, [VMEM] * 4,
        flops=2 * work, bytes_accessed=moved_bytes,
    )
    back = exchange(solve(exchange(sent), gain, high, low))
    error, first = call(
        functools.partial(sweep_kernel, steps), [turned, plane], [SMEM] + [VMEM] * 5,
        flops=2 * work, bytes_accessed=moved_bytes,
    )(step, back, field, excess, high, low)
    last = exchange(solve(exchange(error), gain, high, low))
    increment = call(
        finish_kernel, plane, [VMEM] * 4, flops=work, bytes_accessed=moved_bytes
    )(last, first, high, low)
    return increment[None]


def solution(mesh):
    fine = jax.sharding.Mesh(mesh.devices.reshape(tuple(AXES.values())), tuple(AXES))
    placed = (P(TIME, SLAB, None), P(TIME, SLAB, None), P(SLAB, None), P(SLAB, None))
    return jax.shard_map(
        local, mesh=fine, in_specs=placed, out_specs=P(TIME, SLAB, None), check_vma=False
    )
```

```python
import functools
import math

import jax
import jax.numpy as jnp
import ml_dtypes
import numpy as np
from jax import lax
from jax.experimental import pallas as pl
from jax.experimental.pallas import tpu as pltpu
from jax.sharding import PartitionSpec as P

TIME_STEP = 0.05
CIRCULANT_ALPHA = 0.1
MEAN_DAMPING = 5.25
DAMPING_TABLE = (0.5, 1.0, 1.5, 2.5, 4.0, 6.0, 8.0, 10.0)
AXES = {"xh": 2, "z": 8, "c": 2, "xl": 2, "y": 4}
TIME = ("xh", "z", "c")
SLAB = ("xl", "y")
GROUP = ("xl", "y", "z", "c", "xh")
TILE = 8
SHIFT = 2
VMEM = pl.BlockSpec(memory_space=pltpu.VMEM)
SMEM = pl.BlockSpec(memory_space=pltpu.SMEM)
HBM = pl.BlockSpec(memory_space=pltpu.HBM)


def hartley_tables(length):
    def parts(table):
        table = table / math.sqrt(length)
        high = table.astype(ml_dtypes.bfloat16)
        return high, (table - high.astype(np.float64)).astype(ml_dtypes.bfloat16)

    def cas(angle):
        return np.cos(angle) + np.sin(angle)

    quarter = np.arange(length // 4, dtype=np.int64)
    odd = 2 * quarter + 1
    whole = cas((quarter[:, None] * quarter[None, :] % (length // 4)) * (8.0 * math.pi / length))
    twice = cas((odd[:, None] * odd[None, :] % length) * (2.0 * math.pi / length))
    odd = 2 * np.arange(length // 2, dtype=np.int64) + 1
    half = cas((odd[:, None] * odd[None, :] % (2 * length)) * (math.pi / length))
    return parts(np.concatenate([whole, twice], axis=1)) + parts(half)


def pieces(block):
    high = block.astype(jnp.bfloat16)
    low = (block - high.astype(jnp.float32)).astype(jnp.bfloat16)
    return high, low


def product(a, b, dims):
    return lax.dot_general(a, b, (dims, ((), ())), preferred_element_type=jnp.float32)


def from_right(block, table_high, table_low):
    high, low = pieces(block)
    count = block.shape[0]
    dims = ((1,), (0,))
    tall = product(jnp.concatenate([high, low], axis=0), table_high, dims)
    return tall[:count] + tall[count:] + product(high, table_low, dims)


def transform(block, tables):
    quarter_high, quarter_low, half_high, half_low = tables
    half = half_high.shape[0]
    quarter = half // 2
    left, right = block[:, :half], block[:, half:]
    even, odd = left + right, left - right
    left, right = even[:, :quarter], even[:, quarter:]
    return jnp.concatenate([
        from_right(left + right, quarter_high[:, :quarter], quarter_low[:, :quarter]),
        from_right(left - right, quarter_high[:, quarter:], quarter_low[:, quarter:]),
        from_right(odd, half_high, half_low),
    ], axis=1)


def restore(block, tables):
    quarter_high, quarter_low, half_high, half_low = tables
    half = half_high.shape[0]
    quarter = half // 2
    left = from_right(block[:, :quarter], quarter_high[:, :quarter], quarter_low[:, :quarter])
    right = from_right(block[:, quarter:half], quarter_high[:, quarter:], quarter_low[:, quarter:])
    odd = from_right(block[:, half:], half_high, half_low)
    even = jnp.concatenate([left + right, left - right], axis=1)
    return jnp.concatenate([even + odd, even - odd], axis=1)


def read(tables):
    return [ref[...] for ref in tables]


def excess_of(levels):
    excess = jnp.full(levels.shape, -TIME_STEP * (DAMPING_TABLE[0] - MEAN_DAMPING), jnp.float32)
    for level_id in range(1, len(DAMPING_TABLE)):
        value = -TIME_STEP * (DAMPING_TABLE[level_id] - MEAN_DAMPING)
        excess = jnp.where(levels == level_id, value, excess)
    return excess


def roll(block, amount, axis):
    return pltpu.roll(block, amount % block.shape[axis], axis)


def waves(place, width):
    quarter, half = width // 4, width // 2
    even = jnp.where(place < quarter, 4 * place, 4 * (place - quarter) + 2)
    index = jnp.where(place < half, even, 2 * (place - half) + 1)
    return 4.0 * jnp.sin(index.astype(jnp.float32) * (math.pi / width)) ** 2


def own_terms(x, forcing, levels):
    excess = excess_of(levels)
    grad_cols = roll(x, -1, 1) - roll(x, 1, 1)
    terms = excess * x + TIME_STEP * forcing - (TIME_STEP / 8.0) * (grad_cols * grad_cols)
    return excess, terms


def start_all(pairs, sems):
    copies = [pltpu.make_async_copy(a, b, sems.at[i]) for i, (a, b) in enumerate(pairs)]
    for copy in copies:
        copy.start()
    return copies


def edge_kernel(step_ref, x_hbm, forcing_hbm, initial_hbm, levels_hbm, out_ref,
                x_ref, forcing_ref, initial_ref, levels_ref, sems):
    tile = x_ref.shape[0]
    last = pl.ds(x_hbm.shape[0] - tile, tile)
    copies = start_all([(x_hbm.at[last], x_ref), (forcing_hbm.at[last], forcing_ref),
                        (initial_hbm.at[last], initial_ref), (levels_hbm.at[last], levels_ref)], sems)
    for copy in copies:
        copy.wait()
    x = x_ref[...]
    _, terms = own_terms(x, forcing_ref[...], levels_ref[...])
    out_ref[:tile] = x
    out_ref[tile:] = terms + jnp.where(step_ref[0] == 0, initial_ref[...], 0.0)


def load_kernel(step_ref, column_ref, x_hbm, forcing_hbm, initial_hbm, levels_hbm, *refs):
    count = (len(refs) - 8) // 2
    tables_hbm = refs[:count]
    x_ref, base_ref, excess_ref, gain_ref = refs[count : count + 4]
    tables = refs[count + 4 : 2 * count + 4]
    forcing_ref, initial_ref, levels_ref, sems = refs[2 * count + 4 :]
    copies = start_all(
        [(x_hbm, x_ref), (levels_hbm, levels_ref), (forcing_hbm, forcing_ref), (initial_hbm, initial_ref)]
        + list(zip(tables_hbm, tables)), sems)
    shape = gain_ref.shape
    comps = shape[0] // 2
    lane = lax.broadcasted_iota(jnp.int32, shape, 1)
    row = lax.broadcasted_iota(jnp.int32, shape, 0)
    column = column_ref[0] + jnp.where(row >= comps, row - comps, row)
    modes = waves(lane, shape[1]) + waves(column, shape[1])
    gain_ref[...] = 1.0 / (1.0 + TIME_STEP * (modes * modes - modes + MEAN_DAMPING))
    for copy in copies[:3]:
        copy.wait()
    excess, terms = own_terms(x_ref[...], forcing_ref[...], levels_ref[...])
    excess_ref[...] = excess
    base_ref[...] = terms
    copies[3].wait()

    @pl.when(step_ref[0] == 0)
    def _():
        base_ref[...] += initial_ref[...]

    for copy in copies[4:]:
        copy.wait()


def source_kernel(steps, shift, step_ref, x_ref, base_ref, edge_ref, *refs):
    tables, (out_ref, source_ref) = refs[:-2], refs[-2:]
    rows = x_ref.shape[0]
    tile = edge_ref.shape[0] // 2
    x = jnp.concatenate([edge_ref[:tile], x_ref[...]], axis=0)
    base = jnp.concatenate([edge_ref[tile:], base_ref[...]], axis=0)
    up, down = roll(x, 1, 0), roll(x, -1, 0)
    grad_rows = down - up
    source_ref[...] = base - (TIME_STEP / 8.0) * (grad_rows * grad_rows)

    @pl.when(step_ref[0] == steps - 1)
    def _():
        lap = up + down + roll(x, 1, 1) + roll(x, -1, 1) - 4.0 * x
        lap_two = (
            roll(lap, 1, 0) + roll(lap, -1, 0) + roll(lap, 1, 1) + roll(lap, -1, 1) - 4.0 * lap
        )
        source_ref[...] -= x + TIME_STEP * (lap + lap_two + MEAN_DAMPING * x)

    source = roll(source_ref[...], shift - tile, 0)[:rows]
    out_ref[...] = transform(source, read(tables)).T


def solve_kernel(slabs, steps, shift, x_ref, gain_ref, *refs):
    tables, out_ref = read(refs[:-1]), refs[-1]
    rows = x_ref.shape[0] // slabs
    fields = jnp.concatenate([x_ref[pl.ds(s * rows, rows), :] for s in range(slabs)], axis=1)
    spectrum = transform(fields, tables)
    width = spectrum.shape[1]
    gain = gain_ref[...]
    powers = [gain]
    while len(powers) < steps.bit_length():
        powers.append(powers[-1] * powers[-1])
    start = gain / (1.0 - CIRCULANT_ALPHA * powers[-1])
    pack = gain.shape[0]
    half = pack // 2
    groups = rows // pack
    lane_row = lax.broadcasted_iota(jnp.int32, (1, pack, width), 1)
    u = spectrum.reshape(groups, pack, width) * start[None]

    def around(block):
        turned = roll(block.reshape(-1, width), half, 0).reshape(block.shape)
        if block.shape[0] > 1:
            other = roll(block.reshape(-1, width), -half, 0).reshape(block.shape)
            turned = jnp.where(lane_row < half, other, turned)
        return jnp.where(lane_row < half, CIRCULANT_ALPHA, 1.0) * turned

    for j in range(steps.bit_length() - 1):
        k = 1 << j
        if k < groups:
            moved = jnp.concatenate([around(u[groups - k :]), u[: groups - k]], axis=0)
        else:
            moved = around(u)
        u = u + powers[j][None] * moved
    result = restore(u.reshape(rows, width), tables)
    if shift:
        result = roll(result, -shift, 1)
    for s in range(slabs):
        out_ref[pl.ds(s * rows, rows), :] = result[:, s * rows : (s + 1) * rows]


def sweep_kernel(steps, step_ref, y_ref, x_ref, excess_ref, *refs):
    tables, (out_ref, first_ref) = read(refs[:-2]), refs[-2:]
    keep = jnp.where(step_ref[0] == steps - 1, 0.0, 1.0)
    first = restore(y_ref[...].T, tables) - keep * x_ref[...]
    first_ref[...] = first
    out_ref[...] = transform(excess_ref[...] * first, tables).T


def finish_kernel(y_ref, first_ref, *refs):
    refs[-1][...] = restore(y_ref[...].T, read(refs[:-1])) + first_ref[...]


def call(kernel, out_shapes, specs, scratch=(), flops=0, bytes_accessed=0):
    return pl.pallas_call(
        kernel,
        out_shape=out_shapes,
        in_specs=specs,
        out_specs=[VMEM] * len(out_shapes) if isinstance(out_shapes, (list, tuple)) else VMEM,
        scratch_shapes=list(scratch),
        compiler_params=pltpu.CompilerParams(vmem_limit_bytes=16 * 1024 * 1024),
        cost_estimate=pl.CostEstimate(flops=flops, bytes_accessed=bytes_accessed, transcendentals=0),
    )


def local(iterate, forcing, initial, levels):
    field = iterate[0]
    rows, width = field.shape
    steps, slabs = lax.axis_size(TIME), lax.axis_size(SLAB)
    devices = steps * slabs
    comps = width // devices
    tables = [jnp.asarray(t) for t in hartley_tables(width)]
    step = lax.axis_index(TIME).astype(jnp.int32).reshape(1)
    column = (lax.axis_index(GROUP) * comps).astype(jnp.int32).reshape(1)
    plane = jax.ShapeDtypeStruct((rows, width), jnp.float32)
    turned = jax.ShapeDtypeStruct((width, rows), jnp.float32)
    gains = jax.ShapeDtypeStruct((2 * comps, width), jnp.float32)
    work = 6 * 6 * rows * width * width // 16
    moved_bytes = 2 * width * width + 16 * rows * width

    def exchange(block):
        return lax.all_to_all(
            block.reshape(devices, comps, rows), GROUP, split_axis=0, concat_axis=0, tiled=True
        ).reshape(width, rows)

    stay = [pltpu.with_memory_space_constraint(a, pltpu.HBM)
            for a in (field, forcing[0], initial, levels)]
    stay_tables = [pltpu.with_memory_space_constraint(a, pltpu.HBM) for a in tables]
    buffers = [jnp.float32, jnp.float32, jnp.int32]

    edge = call(
        edge_kernel, jax.ShapeDtypeStruct((2 * TILE, width), jnp.float32), [SMEM] + [HBM] * 4,
        scratch=[pltpu.VMEM((TILE, width), kind) for kind in [jnp.float32] + buffers]
        + [pltpu.SemaphoreType.DMA((4,))],
        flops=32 * TILE * width, bytes_accessed=24 * TILE * width,
    )(step, *stay)
    edge = lax.ppermute(edge, SLAB, [(i, (i + 1) % slabs) for i in range(slabs)])
    field, base, excess, gain, *tables = call(
        load_kernel,
        [plane, plane, plane, gains] + [jax.ShapeDtypeStruct(t.shape, t.dtype) for t in tables],
        [SMEM] * 2 + [HBM] * (4 + len(tables)),
        scratch=[pltpu.VMEM((rows, width), kind) for kind in buffers]
        + [pltpu.SemaphoreType.DMA((4 + len(tables),))],
        flops=32 * rows * width, bytes_accessed=moved_bytes,
    )(step, column, *stay, *stay_tables)
    sent = call(
        functools.partial(source_kernel, steps, SHIFT), turned, [SMEM] + [VMEM] * (3 + len(tables)),
        scratch=[pltpu.VMEM((rows + TILE, width), jnp.float32)], flops=work, bytes_accessed=moved_bytes,
    )(step, field, base, edge, *tables)

    def solve(block, shift):
        return exchange(call(
            functools.partial(solve_kernel, slabs, steps, shift), turned, [VMEM] * (2 + len(tables)),
            flops=2 * work, bytes_accessed=moved_bytes,
        )(exchange(block), gain, *tables))

    error, first = call(
        functools.partial(sweep_kernel, steps), [turned, plane], [SMEM] + [VMEM] * (3 + len(tables)),
        flops=2 * work, bytes_accessed=moved_bytes,
    )(step, solve(sent, SHIFT), field, excess, *tables)
    increment = call(
        finish_kernel, plane, [VMEM] * (2 + len(tables)), flops=work, bytes_accessed=moved_bytes
    )(solve(error, 0), first, *tables)
    return increment[None]


def solution(mesh):
    fine = jax.sharding.Mesh(mesh.devices.reshape(tuple(AXES.values())), tuple(AXES))
    placed = (P(TIME, SLAB, None), P(TIME, SLAB, None), P(SLAB, None), P(SLAB, None))
    return jax.shard_map(
        local, mesh=fine, in_specs=placed, out_specs=P(TIME, SLAB, None), check_vma=False
    )
```

```python
import functools
import math

import jax
import jax.numpy as jnp
import ml_dtypes
import numpy as np
from jax import lax
from jax.experimental import pallas as pl
from jax.experimental.pallas import tpu as pltpu
from jax.sharding import PartitionSpec as P

TIME_STEP = 0.05
CIRCULANT_ALPHA = 0.1
MEAN_DAMPING = 5.25
DAMPING_TABLE = (0.5, 1.0, 1.5, 2.5, 4.0, 6.0, 8.0, 10.0)
AXES = {"xh": 2, "z": 8, "c": 2, "xl": 2, "y": 4}
TIME = ("xh", "z", "c")
SLAB = ("xl", "y")
GROUP = ("xl", "y", "z", "c", "xh")
TILE = 8
SHIFT = 2
VMEM = pl.BlockSpec(memory_space=pltpu.VMEM)
SMEM = pl.BlockSpec(memory_space=pltpu.SMEM)
HBM = pl.BlockSpec(memory_space=pltpu.HBM)


def hartley_tables(length):
    def parts(table):
        table = table / math.sqrt(length)
        high = table.astype(ml_dtypes.bfloat16)
        return high, (table - high.astype(np.float64)).astype(ml_dtypes.bfloat16)

    def cas(angle):
        return np.cos(angle) + np.sin(angle)

    quarter = np.arange(length // 4, dtype=np.int64)
    odd = 2 * quarter + 1
    whole = cas((quarter[:, None] * quarter[None, :] % (length // 4)) * (8.0 * math.pi / length))
    twice = cas((odd[:, None] * odd[None, :] % length) * (2.0 * math.pi / length))
    odd = 2 * np.arange(length // 2, dtype=np.int64) + 1
    half = cas((odd[:, None] * odd[None, :] % (2 * length)) * (math.pi / length))
    return parts(np.concatenate([whole, twice], axis=1)) + parts(half)


def pieces(block):
    high = block.astype(jnp.bfloat16)
    low = (block - high.astype(jnp.float32)).astype(jnp.bfloat16)
    return high, low


def product(a, b, dims):
    return lax.dot_general(a, b, (dims, ((), ())), preferred_element_type=jnp.float32)


def from_right(block, table_high, table_low):
    high, low = pieces(block)
    dims = ((1,), (0,))
    return product(high, table_high, dims) + product(low, table_high, dims) + product(high, table_low, dims)


def transform(block, tables):
    quarter_high, quarter_low, half_high, half_low = tables
    half = half_high.shape[0]
    quarter = half // 2
    left, right = block[:, :half], block[:, half:]
    even, odd = left + right, left - right
    left, right = even[:, :quarter], even[:, quarter:]
    return jnp.concatenate([
        from_right(left + right, quarter_high[:, :quarter], quarter_low[:, :quarter]),
        from_right(left - right, quarter_high[:, quarter:], quarter_low[:, quarter:]),
        from_right(odd, half_high, half_low),
    ], axis=1)


def restore(block, tables):
    quarter_high, quarter_low, half_high, half_low = tables
    half = half_high.shape[0]
    quarter = half // 2
    left = from_right(block[:, :quarter], quarter_high[:, :quarter], quarter_low[:, :quarter])
    right = from_right(block[:, quarter:half], quarter_high[:, quarter:], quarter_low[:, quarter:])
    odd = from_right(block[:, half:], half_high, half_low)
    even = jnp.concatenate([left + right, left - right], axis=1)
    return jnp.concatenate([even + odd, even - odd], axis=1)


def read(tables):
    return [ref[...] for ref in tables]


def excess_of(levels):
    excess = jnp.full(levels.shape, -TIME_STEP * (DAMPING_TABLE[0] - MEAN_DAMPING), jnp.float32)
    for level_id in range(1, len(DAMPING_TABLE)):
        value = -TIME_STEP * (DAMPING_TABLE[level_id] - MEAN_DAMPING)
        excess = jnp.where(levels == level_id, value, excess)
    return excess


def roll(block, amount, axis):
    return pltpu.roll(block, amount % block.shape[axis], axis)


def waves(place, width):
    quarter, half = width // 4, width // 2
    even = jnp.where(place < quarter, 4 * place, 4 * (place - quarter) + 2)
    index = jnp.where(place < half, even, 2 * (place - half) + 1)
    return 4.0 * jnp.sin(index.astype(jnp.float32) * (math.pi / width)) ** 2


def own_terms(x, forcing, levels):
    excess = excess_of(levels)
    grad_cols = roll(x, -1, 1) - roll(x, 1, 1)
    terms = excess * x + TIME_STEP * forcing - (TIME_STEP / 8.0) * (grad_cols * grad_cols)
    return excess, terms


def start_all(pairs, sems):
    copies = [pltpu.make_async_copy(a, b, sems.at[i]) for i, (a, b) in enumerate(pairs)]
    for copy in copies:
        copy.start()
    return copies


def edge_kernel(step_ref, x_hbm, forcing_hbm, initial_hbm, levels_hbm, out_ref,
                x_ref, forcing_ref, initial_ref, levels_ref, sems):
    tile = x_ref.shape[0]
    last = pl.ds(x_hbm.shape[0] - tile, tile)
    copies = start_all([(x_hbm.at[last], x_ref), (forcing_hbm.at[last], forcing_ref),
                        (initial_hbm.at[last], initial_ref), (levels_hbm.at[last], levels_ref)], sems)
    for copy in copies:
        copy.wait()
    x = x_ref[...]
    _, terms = own_terms(x, forcing_ref[...], levels_ref[...])
    terms = terms + jnp.where(step_ref[0] == 0, initial_ref[...], 0.0)
    row = lax.broadcasted_iota(jnp.int32, x.shape, 0)
    out_ref[...] = jnp.where(row < tile // 2, roll(terms, tile // 2, 0), x)


def add_rows(x, last_step, source_ref):
    up, down = roll(x, 1, 0), roll(x, -1, 0)
    grad_rows = down - up
    source_ref[...] -= (TIME_STEP / 8.0) * (grad_rows * grad_rows)

    @pl.when(last_step)
    def _():
        lap = up + down + roll(x, 1, 1) + roll(x, -1, 1) - 4.0 * x
        lap_two = (
            roll(lap, 1, 0) + roll(lap, -1, 0) + roll(lap, 1, 1) + roll(lap, -1, 1) - 4.0 * lap
        )
        source_ref[...] -= x + TIME_STEP * (lap + lap_two + MEAN_DAMPING * x)


def load_kernel(steps, shift, step_ref, column_ref, x_hbm, forcing_hbm, initial_hbm, levels_hbm, *refs):
    count = (len(refs) - 10) // 2
    tables_hbm = refs[:count]
    x_ref, head_ref, ready_ref, excess_ref, gain_ref = refs[count : count + 5]
    tables = refs[count + 5 : 2 * count + 5]
    source_ref, forcing_ref, initial_ref, levels_ref, sems = refs[2 * count + 5 :]
    copies = start_all(
        [(x_hbm, x_ref), (levels_hbm, levels_ref), (forcing_hbm, forcing_ref), (initial_hbm, initial_ref)]
        + list(zip(tables_hbm, tables)), sems)
    shape = gain_ref.shape
    comps = shape[0] // 2
    lane = lax.broadcasted_iota(jnp.int32, shape, 1)
    row = lax.broadcasted_iota(jnp.int32, shape, 0)
    column = column_ref[0] + jnp.where(row >= comps, row - comps, row)
    modes = waves(lane, shape[1]) + waves(column, shape[1])
    gain_ref[...] = 1.0 / (1.0 + TIME_STEP * (modes * modes - modes + MEAN_DAMPING))
    for copy in copies[:3]:
        copy.wait()
    x = x_ref[...]
    excess, terms = own_terms(x, forcing_ref[...], levels_ref[...])
    excess_ref[...] = excess
    source_ref[...] = terms
    copies[3].wait()

    @pl.when(step_ref[0] == 0)
    def _():
        source_ref[...] += initial_ref[...]

    head_ref[...] = source_ref[: head_ref.shape[0]]
    add_rows(x, step_ref[0] == steps - 1, source_ref)
    for copy in copies[4:]:
        copy.wait()
    ready_ref[...] = transform(roll(source_ref[...], shift, 0), read(tables))


def source_kernel(steps, shift, step_ref, x_ref, head_ref, ready_ref, edge_ref, *refs):
    tables, (out_ref, source_ref) = refs[:-2], refs[-2:]
    tile = edge_ref.shape[0]
    edge = edge_ref[...]
    x = jnp.concatenate([edge, x_ref[:tile]], axis=0)
    source_ref[...] = jnp.concatenate([roll(edge, tile // 2, 0), head_ref[...]], axis=0)
    add_rows(x, step_ref[0] == steps - 1, source_ref)
    first = transform(roll(source_ref[...], shift - tile, 0), read(tables))
    out_ref[...] = jnp.concatenate([first[:tile], ready_ref[tile:]], axis=0).T


def solve_kernel(slabs, steps, shift, x_ref, gain_ref, *refs):
    tables, out_ref = read(refs[:-1]), refs[-1]
    rows = x_ref.shape[0] // slabs
    fields = jnp.concatenate([x_ref[pl.ds(s * rows, rows), :] for s in range(slabs)], axis=1)
    spectrum = transform(fields, tables)
    width = spectrum.shape[1]
    gain = gain_ref[...]
    powers = [gain]
    while len(powers) < steps.bit_length():
        powers.append(powers[-1] * powers[-1])
    start = gain / (1.0 - CIRCULANT_ALPHA * powers[-1])
    pack = gain.shape[0]
    half = pack // 2
    groups = rows // pack
    lane_row = lax.broadcasted_iota(jnp.int32, (1, pack, width), 1)
    u = spectrum.reshape(groups, pack, width) * start[None]

    def around(block):
        turned = roll(block.reshape(-1, width), half, 0).reshape(block.shape)
        if block.shape[0] > 1:
            other = roll(block.reshape(-1, width), -half, 0).reshape(block.shape)
            turned = jnp.where(lane_row < half, other, turned)
        return jnp.where(lane_row < half, CIRCULANT_ALPHA, 1.0) * turned

    for j in range(steps.bit_length() - 1):
        k = 1 << j
        if k < groups:
            moved = jnp.concatenate([around(u[groups - k :]), u[: groups - k]], axis=0)
        else:
            moved = around(u)
        u = u + powers[j][None] * moved
    result = restore(u.reshape(rows, width), tables)
    if shift:
        result = roll(result, -shift, 1)
    for s in range(slabs):
        out_ref[pl.ds(s * rows, rows), :] = result[:, s * rows : (s + 1) * rows]


def sweep_kernel(steps, step_ref, y_ref, x_ref, excess_ref, *refs):
    tables, (out_ref, first_ref) = read(refs[:-2]), refs[-2:]
    keep = jnp.where(step_ref[0] == steps - 1, 0.0, 1.0)
    first = restore(y_ref[...].T, tables) - keep * x_ref[...]
    first_ref[...] = first
    out_ref[...] = transform(excess_ref[...] * first, tables).T


def finish_kernel(y_ref, first_ref, *refs):
    refs[-1][...] = restore(y_ref[...].T, read(refs[:-1])) + first_ref[...]


def call(kernel, out_shapes, specs, scratch=(), flops=0, bytes_accessed=0):
    return pl.pallas_call(
        kernel,
        out_shape=out_shapes,
        in_specs=specs,
        out_specs=[VMEM] * len(out_shapes) if isinstance(out_shapes, (list, tuple)) else VMEM,
        scratch_shapes=list(scratch),
        compiler_params=pltpu.CompilerParams(vmem_limit_bytes=16 * 1024 * 1024),
        cost_estimate=pl.CostEstimate(flops=flops, bytes_accessed=bytes_accessed, transcendentals=0),
    )


def local(iterate, forcing, initial, levels):
    field = iterate[0]
    rows, width = field.shape
    steps, slabs = lax.axis_size(TIME), lax.axis_size(SLAB)
    devices = steps * slabs
    comps = width // devices
    tables = [jnp.asarray(t) for t in hartley_tables(width)]
    step = lax.axis_index(TIME).astype(jnp.int32).reshape(1)
    column = (lax.axis_index(GROUP) * comps).astype(jnp.int32).reshape(1)
    plane = jax.ShapeDtypeStruct((rows, width), jnp.float32)
    turned = jax.ShapeDtypeStruct((width, rows), jnp.float32)
    strip = jax.ShapeDtypeStruct((TILE, width), jnp.float32)
    gains = jax.ShapeDtypeStruct((2 * comps, width), jnp.float32)
    work = 6 * 6 * rows * width * width // 16
    moved_bytes = 2 * width * width + 16 * rows * width

    def exchange(block):
        return lax.all_to_all(
            block.reshape(devices, comps, rows), GROUP, split_axis=0, concat_axis=0, tiled=True
        ).reshape(width, rows)

    stay = [pltpu.with_memory_space_constraint(a, pltpu.HBM)
            for a in (field, forcing[0], initial, levels)]
    stay_tables = [pltpu.with_memory_space_constraint(a, pltpu.HBM) for a in tables]
    buffers = [jnp.float32, jnp.float32, jnp.int32]

    edge = call(
        edge_kernel, strip, [SMEM] + [HBM] * 4,
        scratch=[pltpu.VMEM((TILE, width), kind) for kind in [jnp.float32] + buffers]
        + [pltpu.SemaphoreType.DMA((4,))],
        flops=32 * TILE * width, bytes_accessed=24 * TILE * width,
    )(step, *stay)
    edge = lax.ppermute(edge, SLAB, [(i, (i + 1) % slabs) for i in range(slabs)])
    field, head, ready, excess, gain, *tables = call(
        functools.partial(load_kernel, steps, SHIFT),
        [plane, strip, plane, plane, gains] + [jax.ShapeDtypeStruct(t.shape, t.dtype) for t in tables],
        [SMEM] * 2 + [HBM] * (4 + len(tables)),
        scratch=[pltpu.VMEM((rows, width), kind) for kind in [jnp.float32] + buffers]
        + [pltpu.SemaphoreType.DMA((4 + len(tables),))],
        flops=work, bytes_accessed=moved_bytes,
    )(step, column, *stay, *stay_tables)
    sent = call(
        functools.partial(source_kernel, steps, SHIFT), turned, [SMEM] + [VMEM] * (4 + len(tables)),
        scratch=[pltpu.VMEM((2 * TILE, width), jnp.float32)], flops=work, bytes_accessed=moved_bytes,
    )(step, field, head, ready, edge, *tables)

    def solve(block, shift):
        return exchange(call(
            functools.partial(solve_kernel, slabs, steps, shift), turned, [VMEM] * (2 + len(tables)),
            flops=2 * work, bytes_accessed=moved_bytes,
        )(exchange(block), gain, *tables))

    error, first = call(
        functools.partial(sweep_kernel, steps), [turned, plane], [SMEM] + [VMEM] * (3 + len(tables)),
        flops=2 * work, bytes_accessed=moved_bytes,
    )(step, solve(sent, SHIFT), field, excess, *tables)
    increment = call(
        finish_kernel, plane, [VMEM] * (2 + len(tables)), flops=work, bytes_accessed=moved_bytes
    )(solve(error, 0), first, *tables)
    return increment[None]


def solution(mesh):
    fine = jax.sharding.Mesh(mesh.devices.reshape(tuple(AXES.values())), tuple(AXES))
    placed = (P(TIME, SLAB, None), P(TIME, SLAB, None), P(SLAB, None), P(SLAB, None))
    return jax.shard_map(
        local, mesh=fine, in_specs=placed, out_specs=P(TIME, SLAB, None), check_vma=False
    )
```

```python
import functools
import math

import jax
import jax.numpy as jnp
import ml_dtypes
import numpy as np
from jax import lax
from jax.experimental import pallas as pl
from jax.experimental.pallas import tpu as pltpu
from jax.sharding import PartitionSpec as P

TIME_STEP = 0.05
CIRCULANT_ALPHA = 0.1
MEAN_DAMPING = 5.25
DAMPING_TABLE = (0.5, 1.0, 1.5, 2.5, 4.0, 6.0, 8.0, 10.0)
AXES = {"xh": 2, "z": 8, "c": 2, "xl": 2, "y": 4}
TIME = ("xh", "z", "c")
SLAB = ("xl", "y")
GROUP = ("z", "xl", "y")
TILE = 8
SHIFT = 2
VMEM = pl.BlockSpec(memory_space=pltpu.VMEM)
SMEM = pl.BlockSpec(memory_space=pltpu.SMEM)
HBM = pl.BlockSpec(memory_space=pltpu.HBM)


def hartley_tables(length):
    def parts(table):
        table = table / math.sqrt(length)
        high = table.astype(ml_dtypes.bfloat16)
        return high, (table - high.astype(np.float64)).astype(ml_dtypes.bfloat16)

    def cas(angle):
        return np.cos(angle) + np.sin(angle)

    quarter = np.arange(length // 4, dtype=np.int64)
    odd = 2 * quarter + 1
    whole = cas((quarter[:, None] * quarter[None, :] % (length // 4)) * (8.0 * math.pi / length))
    twice = cas((odd[:, None] * odd[None, :] % length) * (2.0 * math.pi / length))
    odd = 2 * np.arange(length // 2, dtype=np.int64) + 1
    half = cas((odd[:, None] * odd[None, :] % (2 * length)) * (math.pi / length))
    return parts(np.concatenate([whole, twice], axis=1)) + parts(half)


def pieces(block):
    high = block.astype(jnp.bfloat16)
    low = (block - high.astype(jnp.float32)).astype(jnp.bfloat16)
    return high, low


def product(a, b, dims):
    return lax.dot_general(a, b, (dims, ((), ())), preferred_element_type=jnp.float32)


def from_right(block, table_high, table_low):
    high, low = pieces(block)
    dims = ((1,), (0,))
    return product(high, table_high, dims) + product(low, table_high, dims) + product(high, table_low, dims)


def transform(block, tables):
    quarter_high, quarter_low, half_high, half_low = tables
    half = half_high.shape[0]
    quarter = half // 2
    left, right = block[:, :half], block[:, half:]
    even, odd = left + right, left - right
    left, right = even[:, :quarter], even[:, quarter:]
    return jnp.concatenate([
        from_right(left + right, quarter_high[:, :quarter], quarter_low[:, :quarter]),
        from_right(left - right, quarter_high[:, quarter:], quarter_low[:, quarter:]),
        from_right(odd, half_high, half_low),
    ], axis=1)


def restore(block, tables):
    quarter_high, quarter_low, half_high, half_low = tables
    half = half_high.shape[0]
    quarter = half // 2
    left = from_right(block[:, :quarter], quarter_high[:, :quarter], quarter_low[:, :quarter])
    right = from_right(block[:, quarter:half], quarter_high[:, quarter:], quarter_low[:, quarter:])
    odd = from_right(block[:, half:], half_high, half_low)
    even = jnp.concatenate([left + right, left - right], axis=1)
    return jnp.concatenate([even + odd, even - odd], axis=1)


def read(tables):
    return [ref[...] for ref in tables]


def excess_of(levels):
    excess = jnp.full(levels.shape, -TIME_STEP * (DAMPING_TABLE[0] - MEAN_DAMPING), jnp.float32)
    for level_id in range(1, len(DAMPING_TABLE)):
        value = -TIME_STEP * (DAMPING_TABLE[level_id] - MEAN_DAMPING)
        excess = jnp.where(levels == level_id, value, excess)
    return excess


def roll(block, amount, axis):
    return pltpu.roll(block, amount % block.shape[axis], axis)


def waves(place, width):
    quarter, half = width // 4, width // 2
    even = jnp.where(place < quarter, 4 * place, 4 * (place - quarter) + 2)
    index = jnp.where(place < half, even, 2 * (place - half) + 1)
    return 4.0 * jnp.sin(index.astype(jnp.float32) * (math.pi / width)) ** 2


def own_terms(x, forcing, levels):
    excess = excess_of(levels)
    grad_cols = roll(x, -1, 1) - roll(x, 1, 1)
    terms = excess * x + TIME_STEP * forcing - (TIME_STEP / 8.0) * (grad_cols * grad_cols)
    return excess, terms


def start_all(pairs, sems):
    copies = [pltpu.make_async_copy(a, b, sems.at[i]) for i, (a, b) in enumerate(pairs)]
    for copy in copies:
        copy.start()
    return copies


def edge_kernel(step_ref, x_hbm, forcing_hbm, initial_hbm, levels_hbm, out_ref,
                x_ref, forcing_ref, initial_ref, levels_ref, sems):
    tile = x_ref.shape[0]
    last = pl.ds(x_hbm.shape[0] - tile, tile)
    copies = start_all([(x_hbm.at[last], x_ref), (forcing_hbm.at[last], forcing_ref),
                        (initial_hbm.at[last], initial_ref), (levels_hbm.at[last], levels_ref)], sems)
    for copy in copies:
        copy.wait()
    x = x_ref[...]
    _, terms = own_terms(x, forcing_ref[...], levels_ref[...])
    terms = terms + jnp.where(step_ref[0] == 0, initial_ref[...], 0.0)
    row = lax.broadcasted_iota(jnp.int32, x.shape, 0)
    out_ref[...] = jnp.where(row < tile // 2, roll(terms, tile // 2, 0), x)


def add_rows(x, last_step, source_ref):
    up, down = roll(x, 1, 0), roll(x, -1, 0)
    grad_rows = down - up
    source_ref[...] -= (TIME_STEP / 8.0) * (grad_rows * grad_rows)

    @pl.when(last_step)
    def _():
        lap = up + down + roll(x, 1, 1) + roll(x, -1, 1) - 4.0 * x
        lap_two = (
            roll(lap, 1, 0) + roll(lap, -1, 0) + roll(lap, 1, 1) + roll(lap, -1, 1) - 4.0 * lap
        )
        source_ref[...] -= x + TIME_STEP * (lap + lap_two + MEAN_DAMPING * x)


def load_kernel(steps, shift, step_ref, column_ref, x_hbm, forcing_hbm, initial_hbm, levels_hbm, *refs):
    count = (len(refs) - 10) // 2
    tables_hbm = refs[:count]
    x_ref, head_ref, ready_ref, excess_ref, gain_ref = refs[count : count + 5]
    tables = refs[count + 5 : 2 * count + 5]
    source_ref, forcing_ref, initial_ref, levels_ref, sems = refs[2 * count + 5 :]
    copies = start_all(
        [(x_hbm, x_ref), (levels_hbm, levels_ref), (forcing_hbm, forcing_ref), (initial_hbm, initial_ref)]
        + list(zip(tables_hbm, tables)), sems)
    shape = gain_ref.shape
    lane = lax.broadcasted_iota(jnp.int32, shape, 1)
    column = column_ref[0] + lax.broadcasted_iota(jnp.int32, shape, 0)
    modes = waves(lane, shape[1]) + waves(column, shape[1])
    gain_ref[...] = 1.0 / (1.0 + TIME_STEP * (modes * modes - modes + MEAN_DAMPING))
    for copy in copies[:3]:
        copy.wait()
    x = x_ref[...]
    excess, terms = own_terms(x, forcing_ref[...], levels_ref[...])
    excess_ref[...] = excess
    source_ref[...] = terms
    copies[3].wait()

    @pl.when(step_ref[0] == 0)
    def _():
        source_ref[...] += initial_ref[...]

    head_ref[...] = source_ref[: head_ref.shape[0]]
    add_rows(x, step_ref[0] == steps - 1, source_ref)
    for copy in copies[4:]:
        copy.wait()
    ready_ref[...] = transform(roll(source_ref[...], shift, 0), read(tables))


def source_kernel(steps, shift, step_ref, x_ref, head_ref, ready_ref, edge_ref, *refs):
    tables, (out_ref, source_ref) = refs[:-2], refs[-2:]
    tile = edge_ref.shape[0]
    edge = edge_ref[...]
    x = jnp.concatenate([edge, x_ref[:tile]], axis=0)
    source_ref[...] = jnp.concatenate([roll(edge, tile // 2, 0), head_ref[...]], axis=0)
    add_rows(x, step_ref[0] == steps - 1, source_ref)
    first = transform(roll(source_ref[...], shift - tile, 0), read(tables))
    out_ref[...] = jnp.concatenate([first[:tile], ready_ref[tile:]], axis=0).T


def spectrum_kernel(slabs, x_ref, gain_ref, *refs):
    tables, (out_ref, end_ref) = read(refs[:-2]), refs[-2:]
    comps = gain_ref.shape[0]
    blocks = x_ref[...].reshape(-1, slabs, comps, x_ref.shape[1])
    planes = blocks.shape[0]
    fields = jnp.concatenate(
        [blocks[:, s].reshape(planes * comps, -1) for s in range(slabs)], axis=1
    )
    spectrum = transform(fields, tables)
    out_ref[...] = spectrum
    ratio = gain_ref[...] * gain_ref[...]
    end = spectrum[:comps]
    for z in range(1, planes):
        end = spectrum[z * comps : (z + 1) * comps] + ratio * end
    end_ref[...] = end


def solve_kernel(slabs, shift, core_ref, half_ref, own_ref, other_ref, same_ref, cross_ref, gain_ref, *refs):
    tables, out_ref = read(refs[:-1]), refs[-1]
    gain = gain_ref[...]
    comps, width = gain.shape
    planes = own_ref.shape[0] // comps
    first_core = core_ref[0] == 0
    ratio = gain * gain
    power = ratio
    for _ in range(planes.bit_length() - 1):
        power = power * power
    own, other = own_ref[...], other_ref[...]
    even, odd = jnp.where(first_core, own, other), jnp.where(first_core, other, own)
    same, cross = same_ref[...], cross_ref[...]
    even_end, odd_end = jnp.where(first_core, same, cross), jnp.where(first_core, cross, same)
    even = [even[z * comps : (z + 1) * comps] for z in range(planes)]
    pairs = [gain * odd[z * comps : (z + 1) * comps] + ratio * even[z] for z in range(planes)]
    own_end = pairs[0]
    for z in range(1, planes):
        own_end = pairs[z] + ratio * own_end
    other_end = gain * odd_end + ratio * even_end
    weight = jnp.where(half_ref[0] == 0, CIRCULANT_ALPHA, 1.0)
    before = (weight * other_end + CIRCULANT_ALPHA * power * own_end) / (
        1.0 - CIRCULANT_ALPHA * power * power
    )
    solved = []
    for z in range(planes):
        after = pairs[z] + ratio * before
        solved.append(jnp.where(first_core, gain * (even[z] + before), after))
        before = after
    result = restore(jnp.concatenate(solved, axis=0), tables)
    if shift:
        result = roll(result, -shift, 1)
    rows = width // slabs
    for s in range(slabs):
        part = result[:, s * rows : (s + 1) * rows]
        for z in range(planes):
            out_ref[pl.ds((z * slabs + s) * comps, comps), :] = part[z * comps : (z + 1) * comps]


def sweep_kernel(steps, step_ref, y_ref, x_ref, excess_ref, *refs):
    tables, (out_ref, first_ref) = read(refs[:-2]), refs[-2:]
    keep = jnp.where(step_ref[0] == steps - 1, 0.0, 1.0)
    first = restore(y_ref[...].T, tables) - keep * x_ref[...]
    first_ref[...] = first
    out_ref[...] = transform(excess_ref[...] * first, tables).T


def finish_kernel(y_ref, first_ref, *refs):
    refs[-1][...] = restore(y_ref[...].T, read(refs[:-1])) + first_ref[...]


def call(kernel, out_shapes, specs, scratch=(), flops=0, bytes_accessed=0):
    return pl.pallas_call(
        kernel,
        out_shape=out_shapes,
        in_specs=specs,
        out_specs=[VMEM] * len(out_shapes) if isinstance(out_shapes, (list, tuple)) else VMEM,
        scratch_shapes=list(scratch),
        compiler_params=pltpu.CompilerParams(vmem_limit_bytes=16 * 1024 * 1024),
        cost_estimate=pl.CostEstimate(flops=flops, bytes_accessed=bytes_accessed, transcendentals=0),
    )


def local(iterate, forcing, initial, levels):
    field = iterate[0]
    rows, width = field.shape
    steps, slabs, peers = (lax.axis_size(axes) for axes in (TIME, SLAB, GROUP))
    comps = width // peers
    tables = [jnp.asarray(t) for t in hartley_tables(width)]
    step = lax.axis_index(TIME).astype(jnp.int32).reshape(1)
    column = (lax.axis_index(GROUP) * comps).astype(jnp.int32).reshape(1)
    plane = jax.ShapeDtypeStruct((rows, width), jnp.float32)
    turned = jax.ShapeDtypeStruct((width, rows), jnp.float32)
    strip = jax.ShapeDtypeStruct((TILE, width), jnp.float32)
    gains = jax.ShapeDtypeStruct((comps, width), jnp.float32)
    work = 6 * 6 * rows * width * width // 16
    moved_bytes = 2 * width * width + 16 * rows * width

    def exchange(block):
        return lax.all_to_all(
            block.reshape(peers, comps, rows), GROUP, split_axis=0, concat_axis=0, tiled=True
        ).reshape(width, rows)

    stay = [pltpu.with_memory_space_constraint(a, pltpu.HBM)
            for a in (field, forcing[0], initial, levels)]
    stay_tables = [pltpu.with_memory_space_constraint(a, pltpu.HBM) for a in tables]
    buffers = [jnp.float32, jnp.float32, jnp.int32]

    edge = call(
        edge_kernel, strip, [SMEM] + [HBM] * 4,
        scratch=[pltpu.VMEM((TILE, width), kind) for kind in [jnp.float32] + buffers]
        + [pltpu.SemaphoreType.DMA((4,))],
        flops=32 * TILE * width, bytes_accessed=24 * TILE * width,
    )(step, *stay)
    edge = lax.ppermute(edge, SLAB, [(i, (i + 1) % slabs) for i in range(slabs)])
    field, head, ready, excess, gain, *tables = call(
        functools.partial(load_kernel, steps, SHIFT),
        [plane, strip, plane, plane, gains] + [jax.ShapeDtypeStruct(t.shape, t.dtype) for t in tables],
        [SMEM] * 2 + [HBM] * (4 + len(tables)),
        scratch=[pltpu.VMEM((rows, width), kind) for kind in [jnp.float32] + buffers]
        + [pltpu.SemaphoreType.DMA((4 + len(tables),))],
        flops=work, bytes_accessed=moved_bytes,
    )(step, column, *stay, *stay_tables)
    sent = call(
        functools.partial(source_kernel, steps, SHIFT), turned, [SMEM] + [VMEM] * (4 + len(tables)),
        scratch=[pltpu.VMEM((2 * TILE, width), jnp.float32)], flops=work, bytes_accessed=moved_bytes,
    )(step, field, head, ready, edge, *tables)

    core, half = (lax.axis_index(axis).astype(jnp.int32).reshape(1) for axis in ("c", "xh"))
    swap = [(0, 1), (1, 0)]

    def solve(block, shift):
        own, end = call(
            functools.partial(spectrum_kernel, slabs), [plane, gains], [VMEM] * (2 + len(tables)),
            flops=work, bytes_accessed=moved_bytes,
        )(exchange(block), gain, *tables)
        same = lax.ppermute(end, "xh", swap)
        cross = lax.ppermute(end, ("xh", "c"), [(i, 3 - i) for i in range(4)])
        other = lax.ppermute(own, "c", swap)
        return exchange(call(
            functools.partial(solve_kernel, slabs, shift), turned,
            [SMEM] * 2 + [VMEM] * (5 + len(tables)), flops=work, bytes_accessed=moved_bytes,
        )(core, half, own, other, same, cross, gain, *tables))

    error, first = call(
        functools.partial(sweep_kernel, steps), [turned, plane], [SMEM] + [VMEM] * (3 + len(tables)),
        flops=2 * work, bytes_accessed=moved_bytes,
    )(step, solve(sent, SHIFT), field, excess, *tables)
    increment = call(
        finish_kernel, plane, [VMEM] * (2 + len(tables)), flops=work, bytes_accessed=moved_bytes
    )(solve(error, 0), first, *tables)
    return increment[None]


def solution(mesh):
    fine = jax.sharding.Mesh(mesh.devices.reshape(tuple(AXES.values())), tuple(AXES))
    placed = (P(TIME, SLAB, None), P(TIME, SLAB, None), P(SLAB, None), P(SLAB, None))
    return jax.shard_map(
        local, mesh=fine, in_specs=placed, out_specs=P(TIME, SLAB, None), check_vma=False
    )
```

```python
import functools
import math

import jax
import jax.numpy as jnp
import ml_dtypes
import numpy as np
from jax import lax
from jax.experimental import pallas as pl
from jax.experimental.pallas import tpu as pltpu
from jax.sharding import PartitionSpec as P

TIME_STEP = 0.05
CIRCULANT_ALPHA = 0.1
MEAN_DAMPING = 5.25
DAMPING_TABLE = (0.5, 1.0, 1.5, 2.5, 4.0, 6.0, 8.0, 10.0)
AXES = {"xh": 2, "z": 8, "c": 2, "xl": 2, "y": 4}
TIME = ("xh", "z", "c")
SLAB = ("xl", "y")
GROUP = ("z", "xl", "y", "xh")
TILE = 8
SHIFT = 2
VMEM = pl.BlockSpec(memory_space=pltpu.VMEM)
SMEM = pl.BlockSpec(memory_space=pltpu.SMEM)
HBM = pl.BlockSpec(memory_space=pltpu.HBM)


def hartley_tables(length):
    def parts(table):
        table = table / math.sqrt(length)
        high = table.astype(ml_dtypes.bfloat16)
        return high, (table - high.astype(np.float64)).astype(ml_dtypes.bfloat16)

    def cas(angle):
        return np.cos(angle) + np.sin(angle)

    quarter = np.arange(length // 4, dtype=np.int64)
    odd = 2 * quarter + 1
    whole = cas((quarter[:, None] * quarter[None, :] % (length // 4)) * (8.0 * math.pi / length))
    twice = cas((odd[:, None] * odd[None, :] % length) * (2.0 * math.pi / length))
    odd = 2 * np.arange(length // 2, dtype=np.int64) + 1
    half = cas((odd[:, None] * odd[None, :] % (2 * length)) * (math.pi / length))
    return parts(np.concatenate([whole, twice], axis=1)) + parts(half)


def pieces(block):
    high = block.astype(jnp.bfloat16)
    low = (block - high.astype(jnp.float32)).astype(jnp.bfloat16)
    return high, low


def product(a, b, dims):
    return lax.dot_general(a, b, (dims, ((), ())), preferred_element_type=jnp.float32)


def from_right(block, table_high, table_low):
    high, low = pieces(block)
    dims = ((1,), (0,))
    return product(high, table_high, dims) + product(low, table_high, dims) + product(high, table_low, dims)


def transform(block, tables):
    quarter_high, quarter_low, half_high, half_low = tables
    half = half_high.shape[0]
    quarter = half // 2
    left, right = block[:, :half], block[:, half:]
    even, odd = left + right, left - right
    left, right = even[:, :quarter], even[:, quarter:]
    return jnp.concatenate([
        from_right(left + right, quarter_high[:, :quarter], quarter_low[:, :quarter]),
        from_right(left - right, quarter_high[:, quarter:], quarter_low[:, quarter:]),
        from_right(odd, half_high, half_low),
    ], axis=1)


def restore(block, tables):
    quarter_high, quarter_low, half_high, half_low = tables
    half = half_high.shape[0]
    quarter = half // 2
    left = from_right(block[:, :quarter], quarter_high[:, :quarter], quarter_low[:, :quarter])
    right = from_right(block[:, quarter:half], quarter_high[:, quarter:], quarter_low[:, quarter:])
    odd = from_right(block[:, half:], half_high, half_low)
    even = jnp.concatenate([left + right, left - right], axis=1)
    return jnp.concatenate([even + odd, even - odd], axis=1)


def read(tables):
    return [ref[...] for ref in tables]


def excess_of(levels):
    excess = jnp.full(levels.shape, -TIME_STEP * (DAMPING_TABLE[0] - MEAN_DAMPING), jnp.float32)
    for level_id in range(1, len(DAMPING_TABLE)):
        value = -TIME_STEP * (DAMPING_TABLE[level_id] - MEAN_DAMPING)
        excess = jnp.where(levels == level_id, value, excess)
    return excess


def roll(block, amount, axis):
    return pltpu.roll(block, amount % block.shape[axis], axis)


def waves(place, width):
    quarter, half = width // 4, width // 2
    even = jnp.where(place < quarter, 4 * place, 4 * (place - quarter) + 2)
    index = jnp.where(place < half, even, 2 * (place - half) + 1)
    return 4.0 * jnp.sin(index.astype(jnp.float32) * (math.pi / width)) ** 2


def own_terms(x, forcing, levels):
    excess = excess_of(levels)
    grad_cols = roll(x, -1, 1) - roll(x, 1, 1)
    terms = excess * x + TIME_STEP * forcing - (TIME_STEP / 8.0) * (grad_cols * grad_cols)
    return excess, terms


def start_all(pairs, sems):
    copies = [pltpu.make_async_copy(a, b, sems.at[i]) for i, (a, b) in enumerate(pairs)]
    for copy in copies:
        copy.start()
    return copies


def edge_kernel(step_ref, x_hbm, forcing_hbm, initial_hbm, levels_hbm, out_ref,
                x_ref, forcing_ref, initial_ref, levels_ref, sems):
    tile = x_ref.shape[0]
    last = pl.ds(x_hbm.shape[0] - tile, tile)
    copies = start_all([(x_hbm.at[last], x_ref), (forcing_hbm.at[last], forcing_ref),
                        (initial_hbm.at[last], initial_ref), (levels_hbm.at[last], levels_ref)], sems)
    for copy in copies:
        copy.wait()
    x = x_ref[...]
    _, terms = own_terms(x, forcing_ref[...], levels_ref[...])
    terms = terms + jnp.where(step_ref[0] == 0, initial_ref[...], 0.0)
    row = lax.broadcasted_iota(jnp.int32, x.shape, 0)
    out_ref[...] = jnp.where(row < tile // 2, roll(terms, tile // 2, 0), x)


def add_rows(x, last_step, source_ref):
    up, down = roll(x, 1, 0), roll(x, -1, 0)
    grad_rows = down - up
    source_ref[...] -= (TIME_STEP / 8.0) * (grad_rows * grad_rows)

    @pl.when(last_step)
    def _():
        lap = up + down + roll(x, 1, 1) + roll(x, -1, 1) - 4.0 * x
        lap_two = (
            roll(lap, 1, 0) + roll(lap, -1, 0) + roll(lap, 1, 1) + roll(lap, -1, 1) - 4.0 * lap
        )
        source_ref[...] -= x + TIME_STEP * (lap + lap_two + MEAN_DAMPING * x)


def load_kernel(steps, shift, step_ref, column_ref, x_hbm, forcing_hbm, initial_hbm, levels_hbm, *refs):
    count = (len(refs) - 10) // 2
    tables_hbm = refs[:count]
    x_ref, head_ref, ready_ref, excess_ref, gain_ref = refs[count : count + 5]
    tables = refs[count + 5 : 2 * count + 5]
    source_ref, forcing_ref, initial_ref, levels_ref, sems = refs[2 * count + 5 :]
    copies = start_all(
        [(x_hbm, x_ref), (levels_hbm, levels_ref), (forcing_hbm, forcing_ref), (initial_hbm, initial_ref)]
        + list(zip(tables_hbm, tables)), sems)
    shape = gain_ref.shape
    lane = lax.broadcasted_iota(jnp.int32, shape, 1)
    column = column_ref[0] + lax.broadcasted_iota(jnp.int32, shape, 0)
    modes = waves(lane, shape[1]) + waves(column, shape[1])
    gain_ref[...] = 1.0 / (1.0 + TIME_STEP * (modes * modes - modes + MEAN_DAMPING))
    for copy in copies[:3]:
        copy.wait()
    x = x_ref[...]
    excess, terms = own_terms(x, forcing_ref[...], levels_ref[...])
    excess_ref[...] = excess
    source_ref[...] = terms
    copies[3].wait()

    @pl.when(step_ref[0] == 0)
    def _():
        source_ref[...] += initial_ref[...]

    head_ref[...] = source_ref[: head_ref.shape[0]]
    add_rows(x, step_ref[0] == steps - 1, source_ref)
    for copy in copies[4:]:
        copy.wait()
    ready_ref[...] = transform(roll(source_ref[...], shift, 0), read(tables))


def source_kernel(steps, shift, step_ref, x_ref, head_ref, ready_ref, edge_ref, *refs):
    tables, (out_ref, source_ref) = refs[:-2], refs[-2:]
    tile = edge_ref.shape[0]
    edge = edge_ref[...]
    x = jnp.concatenate([edge, x_ref[:tile]], axis=0)
    source_ref[...] = jnp.concatenate([roll(edge, tile // 2, 0), head_ref[...]], axis=0)
    add_rows(x, step_ref[0] == steps - 1, source_ref)
    first = transform(roll(source_ref[...], shift - tile, 0), read(tables))
    out_ref[...] = jnp.concatenate([first[:tile], ready_ref[tile:]], axis=0).T


def spectrum_kernel(slabs, planes, x_ref, *refs):
    tables, out_ref = read(refs[:-1]), refs[-1]
    blocks = x_ref[...].reshape(planes, slabs, -1, x_ref.shape[1])
    fields = jnp.concatenate(
        [blocks[:, s].reshape(-1, x_ref.shape[1]) for s in range(slabs)], axis=1
    )
    out_ref[...] = transform(fields, tables)


def solve_kernel(slabs, planes, shift, core_ref, own_ref, other_ref, gain_ref, *refs):
    tables, out_ref = read(refs[:-1]), refs[-1]
    gain = gain_ref[...]
    comps, width = gain.shape
    count = own_ref.shape[0] // comps
    halves = count // planes
    first_core = core_ref[0] == 0
    ratio = gain * gain
    power = ratio
    for _ in range(count.bit_length() - 1):
        power = power * power
    own, other = own_ref[...], other_ref[...]
    even, odd = jnp.where(first_core, own, other), jnp.where(first_core, other, own)
    order = [z * halves + half for half in range(halves) for z in range(planes)]
    even = [even[i * comps : (i + 1) * comps] for i in order]
    pairs = [gain * odd[i * comps : (i + 1) * comps] + ratio * e for i, e in zip(order, even)]
    end = pairs[0]
    for pair in pairs[1:]:
        end = pair + ratio * end
    before = end * (CIRCULANT_ALPHA / (1.0 - CIRCULANT_ALPHA * power))
    solved = [None] * count
    for i, pair, e in zip(order, pairs, even):
        after = pair + ratio * before
        solved[i] = jnp.where(first_core, gain * (e + before), after)
        before = after
    result = restore(jnp.concatenate(solved, axis=0), tables)
    if shift:
        result = roll(result, -shift, 1)
    rows, chunk = width // slabs, halves * comps
    for s in range(slabs):
        part = result[:, s * rows : (s + 1) * rows]
        for z in range(planes):
            out_ref[pl.ds((z * slabs + s) * chunk, chunk), :] = part[z * chunk : (z + 1) * chunk]


def sweep_kernel(steps, step_ref, y_ref, x_ref, excess_ref, *refs):
    tables, (out_ref, first_ref) = read(refs[:-2]), refs[-2:]
    keep = jnp.where(step_ref[0] == steps - 1, 0.0, 1.0)
    first = restore(y_ref[...].T, tables) - keep * x_ref[...]
    first_ref[...] = first
    out_ref[...] = transform(excess_ref[...] * first, tables).T


def finish_kernel(y_ref, first_ref, *refs):
    refs[-1][...] = restore(y_ref[...].T, read(refs[:-1])) + first_ref[...]


def call(kernel, out_shapes, specs, scratch=(), flops=0, bytes_accessed=0):
    return pl.pallas_call(
        kernel,
        out_shape=out_shapes,
        in_specs=specs,
        out_specs=[VMEM] * len(out_shapes) if isinstance(out_shapes, (list, tuple)) else VMEM,
        scratch_shapes=list(scratch),
        compiler_params=pltpu.CompilerParams(vmem_limit_bytes=16 * 1024 * 1024),
        cost_estimate=pl.CostEstimate(flops=flops, bytes_accessed=bytes_accessed, transcendentals=0),
    )


def local(iterate, forcing, initial, levels):
    field = iterate[0]
    rows, width = field.shape
    steps, slabs, peers = (lax.axis_size(axes) for axes in (TIME, SLAB, GROUP))
    comps = width // peers
    tables = [jnp.asarray(t) for t in hartley_tables(width)]
    step = lax.axis_index(TIME).astype(jnp.int32).reshape(1)
    column = (lax.axis_index(GROUP) * comps).astype(jnp.int32).reshape(1)
    plane = jax.ShapeDtypeStruct((rows, width), jnp.float32)
    turned = jax.ShapeDtypeStruct((width, rows), jnp.float32)
    strip = jax.ShapeDtypeStruct((TILE, width), jnp.float32)
    gains = jax.ShapeDtypeStruct((comps, width), jnp.float32)
    work = 6 * 6 * rows * width * width // 16
    moved_bytes = 2 * width * width + 16 * rows * width

    def exchange(block):
        return lax.all_to_all(
            block.reshape(peers, comps, rows), GROUP, split_axis=0, concat_axis=0, tiled=True
        ).reshape(width, rows)

    stay = [pltpu.with_memory_space_constraint(a, pltpu.HBM)
            for a in (field, forcing[0], initial, levels)]
    stay_tables = [pltpu.with_memory_space_constraint(a, pltpu.HBM) for a in tables]
    buffers = [jnp.float32, jnp.float32, jnp.int32]

    edge = call(
        edge_kernel, strip, [SMEM] + [HBM] * 4,
        scratch=[pltpu.VMEM((TILE, width), kind) for kind in [jnp.float32] + buffers]
        + [pltpu.SemaphoreType.DMA((4,))],
        flops=32 * TILE * width, bytes_accessed=24 * TILE * width,
    )(step, *stay)
    edge = lax.ppermute(edge, SLAB, [(i, (i + 1) % slabs) for i in range(slabs)])
    field, head, ready, excess, gain, *tables = call(
        functools.partial(load_kernel, steps, SHIFT),
        [plane, strip, plane, plane, gains] + [jax.ShapeDtypeStruct(t.shape, t.dtype) for t in tables],
        [SMEM] * 2 + [HBM] * (4 + len(tables)),
        scratch=[pltpu.VMEM((rows, width), kind) for kind in [jnp.float32] + buffers]
        + [pltpu.SemaphoreType.DMA((4 + len(tables),))],
        flops=work, bytes_accessed=moved_bytes,
    )(step, column, *stay, *stay_tables)
    sent = call(
        functools.partial(source_kernel, steps, SHIFT), turned, [SMEM] + [VMEM] * (4 + len(tables)),
        scratch=[pltpu.VMEM((2 * TILE, width), jnp.float32)], flops=work, bytes_accessed=moved_bytes,
    )(step, field, head, ready, edge, *tables)

    core = lax.axis_index("c").astype(jnp.int32).reshape(1)
    planes = lax.axis_size("z")

    def solve(block, shift):
        own = call(
            functools.partial(spectrum_kernel, slabs, planes), plane, [VMEM] * (1 + len(tables)),
            flops=work, bytes_accessed=moved_bytes,
        )(exchange(block), *tables)
        other = lax.ppermute(own, "c", [(0, 1), (1, 0)])
        return exchange(call(
            functools.partial(solve_kernel, slabs, planes, shift), turned,
            [SMEM] + [VMEM] * (3 + len(tables)), flops=work, bytes_accessed=moved_bytes,
        )(core, own, other, gain, *tables))

    error, first = call(
        functools.partial(sweep_kernel, steps), [turned, plane], [SMEM] + [VMEM] * (3 + len(tables)),
        flops=2 * work, bytes_accessed=moved_bytes,
    )(step, solve(sent, SHIFT), field, excess, *tables)
    increment = call(
        finish_kernel, plane, [VMEM] * (2 + len(tables)), flops=work, bytes_accessed=moved_bytes
    )(solve(error, 0), first, *tables)
    return increment[None]


def solution(mesh):
    fine = jax.sharding.Mesh(mesh.devices.reshape(tuple(AXES.values())), tuple(AXES))
    placed = (P(TIME, SLAB, None), P(TIME, SLAB, None), P(SLAB, None), P(SLAB, None))
    return jax.shard_map(
        local, mesh=fine, in_specs=placed, out_specs=P(TIME, SLAB, None), check_vma=False
    )
```

```python
import functools
import math

import jax
import jax.numpy as jnp
import ml_dtypes
import numpy as np
from jax import lax
from jax.experimental import pallas as pl
from jax.experimental.pallas import tpu as pltpu
from jax.sharding import PartitionSpec as P

TIME_STEP = 0.05
CIRCULANT_ALPHA = 0.1
MEAN_DAMPING = 5.25
DAMPING_TABLE = (0.5, 1.0, 1.5, 2.5, 4.0, 6.0, 8.0, 10.0)
AXES = {"xh": 2, "z": 8, "c": 2, "xl": 2, "y": 4}
TIME = ("xh", "z", "c")
SLAB = ("xl", "y")
GROUP = ("xl", "y", "z", "c", "xh")
TILE = 8
LANES = 128
SHIFT = 2
VMEM = pl.BlockSpec(memory_space=pltpu.VMEM)
SMEM = pl.BlockSpec(memory_space=pltpu.SMEM)
HBM = pl.BlockSpec(memory_space=pltpu.HBM)


def hartley_tables(length):
    def parts(table):
        table = table / math.sqrt(length)
        high = table.astype(ml_dtypes.bfloat16)
        return high, (table - high.astype(np.float64)).astype(ml_dtypes.bfloat16)

    def cas(angle):
        return np.cos(angle) + np.sin(angle)

    quarter = np.arange(length // 4, dtype=np.int64)
    odd = 2 * quarter + 1
    whole = cas((quarter[:, None] * quarter[None, :] % (length // 4)) * (8.0 * math.pi / length))
    twice = cas((odd[:, None] * odd[None, :] % length) * (2.0 * math.pi / length))
    odd = 2 * np.arange(length // 2, dtype=np.int64) + 1
    half = cas((odd[:, None] * odd[None, :] % (2 * length)) * (math.pi / length))
    return parts(np.concatenate([whole, twice], axis=1)) + parts(half)


def pieces(block):
    high = block.astype(jnp.bfloat16)
    low = (block - high.astype(jnp.float32)).astype(jnp.bfloat16)
    return high, low


def product(a, b, dims):
    return lax.dot_general(a, b, (dims, ((), ())), preferred_element_type=jnp.float32)


def from_right(block, table_high, table_low):
    high, low = pieces(block)
    dims = ((1,), (0,))
    return product(high, table_high, dims) + product(low, table_high, dims) + product(high, table_low, dims)


def transform(block, tables):
    quarter_high, quarter_low, half_high, half_low = tables
    half = half_high.shape[0]
    quarter = half // 2
    left, right = block[:, :half], block[:, half:]
    even, odd = left + right, left - right
    left, right = even[:, :quarter], even[:, quarter:]
    return jnp.concatenate([
        from_right(left + right, quarter_high[:, :quarter], quarter_low[:, :quarter]),
        from_right(left - right, quarter_high[:, quarter:], quarter_low[:, quarter:]),
        from_right(odd, half_high, half_low),
    ], axis=1)


def restore(block, tables):
    quarter_high, quarter_low, half_high, half_low = tables
    half = half_high.shape[0]
    quarter = half // 2
    left = from_right(block[:, :quarter], quarter_high[:, :quarter], quarter_low[:, :quarter])
    right = from_right(block[:, quarter:half], quarter_high[:, quarter:], quarter_low[:, quarter:])
    odd = from_right(block[:, half:], half_high, half_low)
    even = jnp.concatenate([left + right, left - right], axis=1)
    return jnp.concatenate([even + odd, even - odd], axis=1)


def read(tables):
    return [ref[...] for ref in tables]


def excess_of(levels):
    excess = jnp.full(levels.shape, -TIME_STEP * (DAMPING_TABLE[0] - MEAN_DAMPING), jnp.float32)
    for level_id in range(1, len(DAMPING_TABLE)):
        value = -TIME_STEP * (DAMPING_TABLE[level_id] - MEAN_DAMPING)
        excess = jnp.where(levels == level_id, value, excess)
    return excess


def roll(block, amount, axis):
    return pltpu.roll(block, amount % block.shape[axis], axis)


def waves(place, width):
    quarter, half = width // 4, width // 2
    even = jnp.where(place < quarter, 4 * place, 4 * (place - quarter) + 2)
    index = jnp.where(place < half, even, 2 * (place - half) + 1)
    return 4.0 * jnp.sin(index.astype(jnp.float32) * (math.pi / width)) ** 2


def own_terms(x, forcing, levels):
    excess = excess_of(levels)
    grad_cols = roll(x, -1, 1) - roll(x, 1, 1)
    terms = excess * x + TIME_STEP * forcing - (TIME_STEP / 8.0) * (grad_cols * grad_cols)
    return excess, terms


def start_all(pairs, sems):
    copies = [pltpu.make_async_copy(a, b, sems.at[i]) for i, (a, b) in enumerate(pairs)]
    for copy in copies:
        copy.start()
    return copies


def edge_kernel(step_ref, x_hbm, forcing_hbm, initial_hbm, levels_hbm, out_ref,
                x_ref, forcing_ref, initial_ref, levels_ref, sems):
    tile = x_ref.shape[0]
    last = pl.ds(x_hbm.shape[0] - tile, tile)
    copies = start_all([(x_hbm.at[last], x_ref), (forcing_hbm.at[last], forcing_ref),
                        (initial_hbm.at[last], initial_ref), (levels_hbm.at[last], levels_ref)], sems)
    for copy in copies:
        copy.wait()
    x = x_ref[...]
    _, terms = own_terms(x, forcing_ref[...], levels_ref[...])
    terms = terms + jnp.where(step_ref[0] == 0, initial_ref[...], 0.0)
    row = lax.broadcasted_iota(jnp.int32, x.shape, 0)
    out_ref[...] = jnp.where(row < tile // 2, roll(terms, tile // 2, 0), x)


def add_rows(x, last_step, source_ref):
    up, down = roll(x, 1, 0), roll(x, -1, 0)
    grad_rows = down - up
    source_ref[...] -= (TIME_STEP / 8.0) * (grad_rows * grad_rows)

    @pl.when(last_step)
    def _():
        lap = up + down + roll(x, 1, 1) + roll(x, -1, 1) - 4.0 * x
        lap_two = (
            roll(lap, 1, 0) + roll(lap, -1, 0) + roll(lap, 1, 1) + roll(lap, -1, 1) - 4.0 * lap
        )
        source_ref[...] -= x + TIME_STEP * (lap + lap_two + MEAN_DAMPING * x)


def load_kernel(steps, shift, step_ref, column_ref, x_hbm, forcing_hbm, initial_hbm, levels_hbm, *refs):
    count = (len(refs) - 10) // 2
    tables_hbm = refs[:count]
    x_ref, head_ref, ready_ref, excess_ref, gain_ref = refs[count : count + 5]
    tables = refs[count + 5 : 2 * count + 5]
    source_ref, forcing_ref, initial_ref, levels_ref, sems = refs[2 * count + 5 :]
    copies = start_all(
        [(x_hbm, x_ref), (levels_hbm, levels_ref), (forcing_hbm, forcing_ref)]
        + list(zip(tables_hbm, tables)), sems)
    late = pltpu.make_async_copy(initial_hbm, initial_ref, sems.at[len(copies)])

    @pl.when(step_ref[0] == 0)
    def _():
        late.start()

    shape = gain_ref.shape
    comps = shape[0] // 2
    lane = lax.broadcasted_iota(jnp.int32, shape, 1)
    row = lax.broadcasted_iota(jnp.int32, shape, 0)
    column = column_ref[0] + jnp.where(row >= comps, row - comps, row)
    modes = waves(lane, shape[1]) + waves(column, shape[1])
    gain_ref[...] = 1.0 / (1.0 + TIME_STEP * (modes * modes - modes + MEAN_DAMPING))
    for copy in copies[:3]:
        copy.wait()
    x = x_ref[...]
    excess, terms = own_terms(x, forcing_ref[...], levels_ref[...])
    excess_ref[...] = excess
    source_ref[...] = terms

    @pl.when(step_ref[0] == 0)
    def _():
        late.wait()
        source_ref[...] += initial_ref[...]

    head_ref[...] = source_ref[: head_ref.shape[0]]
    add_rows(x, step_ref[0] == steps - 1, source_ref)
    for copy in copies[3:]:
        copy.wait()
    ready_ref[...] = transform(roll(source_ref[...], shift, 0), read(tables)).T


def source_kernel(steps, shift, step_ref, x_ref, head_ref, ready_ref, edge_ref, *refs):
    tables, (out_ref, source_ref) = refs[:-2], refs[-2:]
    tile = edge_ref.shape[0]
    edge = edge_ref[...]
    x = jnp.concatenate([edge, x_ref[:tile]], axis=0)
    source_ref[...] = jnp.concatenate([roll(edge, tile // 2, 0), head_ref[...]], axis=0)
    add_rows(x, step_ref[0] == steps - 1, source_ref)
    first = transform(roll(source_ref[...], shift - tile, 0), read(tables))
    out_ref[...] = ready_ref[...]
    out_ref[:, :tile] = first.T[:, :tile]


def circulate(block, gain, steps):
    rows, lanes = block.shape
    powers = [gain]
    while len(powers) < steps.bit_length():
        powers.append(powers[-1] * powers[-1])
    start = gain / (1.0 - CIRCULANT_ALPHA * powers[-1])
    pack = gain.shape[0]
    half = pack // 2
    groups = rows // pack
    weight = jnp.where(
        lax.broadcasted_iota(jnp.int32, (pack, lanes), 0) < half, CIRCULANT_ALPHA, 1.0
    )
    u = [block[i * pack : (i + 1) * pack] * start for i in range(groups)]
    for j in range(steps.bit_length() - 1):
        k = 1 << j
        around = [weight * roll(part, half, 0) for part in u[groups - min(k, groups) :]]
        moved = around + u[: groups - len(around)]
        u = [part + powers[j] * other for part, other in zip(u, moved)]
    return jnp.concatenate(u, axis=0)


def solve_kernel(slabs, steps, shift, x_ref, gain_ref, *refs):
    tables, out_ref = read(refs[:-1]), refs[-1]
    rows = x_ref.shape[0] // slabs
    fields = jnp.concatenate([x_ref[pl.ds(s * rows, rows), :] for s in range(slabs)], axis=1)
    spectrum = transform(fields, tables)
    width = spectrum.shape[1]
    lanes = min(LANES, width)
    u = jnp.concatenate(
        [circulate(spectrum[:, i : i + lanes], gain_ref[:, i : i + lanes], steps)
         for i in range(0, width, lanes)], axis=1
    )
    result = restore(u, tables)
    if shift:
        result = roll(result, -shift, 1)
    for s in range(slabs):
        out_ref[pl.ds(s * rows, rows), :] = result[:, s * rows : (s + 1) * rows]


def sweep_kernel(steps, step_ref, y_ref, x_ref, excess_ref, *refs):
    tables, (out_ref, first_ref) = read(refs[:-2]), refs[-2:]
    keep = jnp.where(step_ref[0] == steps - 1, 0.0, 1.0)
    first = restore(y_ref[...].T, tables) - keep * x_ref[...]
    first_ref[...] = first
    out_ref[...] = transform(excess_ref[...] * first, tables).T


def finish_kernel(y_ref, first_ref, *refs):
    refs[-1][...] = restore(y_ref[...].T, read(refs[:-1])) + first_ref[...]


def call(kernel, out_shapes, specs, scratch=(), flops=0, bytes_accessed=0):
    return pl.pallas_call(
        kernel,
        out_shape=out_shapes,
        in_specs=specs,
        out_specs=[VMEM] * len(out_shapes) if isinstance(out_shapes, (list, tuple)) else VMEM,
        scratch_shapes=list(scratch),
        compiler_params=pltpu.CompilerParams(vmem_limit_bytes=16 * 1024 * 1024),
        cost_estimate=pl.CostEstimate(flops=flops, bytes_accessed=bytes_accessed, transcendentals=0),
    )


def local(iterate, forcing, initial, levels):
    field = iterate[0]
    rows, width = field.shape
    steps, slabs = lax.axis_size(TIME), lax.axis_size(SLAB)
    devices = steps * slabs
    comps = width // devices
    tables = [jnp.asarray(t) for t in hartley_tables(width)]
    step = lax.axis_index(TIME).astype(jnp.int32).reshape(1)
    column = (lax.axis_index(GROUP) * comps).astype(jnp.int32).reshape(1)
    plane = jax.ShapeDtypeStruct((rows, width), jnp.float32)
    turned = jax.ShapeDtypeStruct((width, rows), jnp.float32)
    strip = jax.ShapeDtypeStruct((TILE, width), jnp.float32)
    gains = jax.ShapeDtypeStruct((2 * comps, width), jnp.float32)
    work = 6 * 6 * rows * width * width // 16
    moved_bytes = 2 * width * width + 16 * rows * width

    def exchange(block):
        return lax.all_to_all(
            block.reshape(devices, comps, rows), GROUP, split_axis=0, concat_axis=0, tiled=True
        ).reshape(width, rows)

    stay = [pltpu.with_memory_space_constraint(a, pltpu.HBM)
            for a in (field, forcing[0], initial, levels)]
    stay_tables = [pltpu.with_memory_space_constraint(a, pltpu.HBM) for a in tables]
    buffers = [jnp.float32, jnp.float32, jnp.int32]

    edge = call(
        edge_kernel, strip, [SMEM] + [HBM] * 4,
        scratch=[pltpu.VMEM((TILE, width), kind) for kind in [jnp.float32] + buffers]
        + [pltpu.SemaphoreType.DMA((4,))],
        flops=32 * TILE * width, bytes_accessed=24 * TILE * width,
    )(step, *stay)
    edge = lax.ppermute(edge, SLAB, [(i, (i + 1) % slabs) for i in range(slabs)])
    field, head, ready, excess, gain, *tables = call(
        functools.partial(load_kernel, steps, SHIFT),
        [plane, strip, turned, plane, gains] + [jax.ShapeDtypeStruct(t.shape, t.dtype) for t in tables],
        [SMEM] * 2 + [HBM] * (4 + len(tables)),
        scratch=[pltpu.VMEM((rows, width), kind) for kind in [jnp.float32] + buffers]
        + [pltpu.SemaphoreType.DMA((4 + len(tables),))],
        flops=work, bytes_accessed=moved_bytes,
    )(step, column, *stay, *stay_tables)
    sent = call(
        functools.partial(source_kernel, steps, SHIFT), turned, [SMEM] + [VMEM] * (4 + len(tables)),
        scratch=[pltpu.VMEM((2 * TILE, width), jnp.float32)], flops=work, bytes_accessed=moved_bytes,
    )(step, field, head, ready, edge, *tables)

    def solve(block, shift):
        return exchange(call(
            functools.partial(solve_kernel, slabs, steps, shift), turned, [VMEM] * (2 + len(tables)),
            flops=2 * work, bytes_accessed=moved_bytes,
        )(exchange(block), gain, *tables))

    error, first = call(
        functools.partial(sweep_kernel, steps), [turned, plane], [SMEM] + [VMEM] * (3 + len(tables)),
        flops=2 * work, bytes_accessed=moved_bytes,
    )(step, solve(sent, SHIFT), field, excess, *tables)
    increment = call(
        finish_kernel, plane, [VMEM] * (2 + len(tables)), flops=work, bytes_accessed=moved_bytes
    )(solve(error, 0), first, *tables)
    return increment[None]


def solution(mesh):
    fine = jax.sharding.Mesh(mesh.devices.reshape(tuple(AXES.values())), tuple(AXES))
    placed = (P(TIME, SLAB, None), P(TIME, SLAB, None), P(SLAB, None), P(SLAB, None))
    return jax.shard_map(
        local, mesh=fine, in_specs=placed, out_specs=P(TIME, SLAB, None), check_vma=False
    )
```

```python
import functools
import math

import jax
import jax.numpy as jnp
import ml_dtypes
import numpy as np
from jax import lax
from jax.experimental import pallas as pl
from jax.experimental.pallas import tpu as pltpu
from jax.sharding import PartitionSpec as P

TIME_STEP = 0.05
CIRCULANT_ALPHA = 0.1
MEAN_DAMPING = 5.25
DAMPING_TABLE = (0.5, 1.0, 1.5, 2.5, 4.0, 6.0, 8.0, 10.0)
AXES = {"xh": 2, "z": 8, "c": 2, "xl": 2, "y": 4}
TIME = ("xh", "z", "c")
SLAB = ("xl", "y")
GROUP = ("xl", "y", "z", "c", "xh")
TILE = 8
LANES = 128
SHIFT = 2
VMEM = pl.BlockSpec(memory_space=pltpu.VMEM)
SMEM = pl.BlockSpec(memory_space=pltpu.SMEM)
HBM = pl.BlockSpec(memory_space=pltpu.HBM)


def hartley_tables(length):
    def parts(table):
        table = table / math.sqrt(length)
        high = table.astype(ml_dtypes.bfloat16)
        return high, (table - high.astype(np.float64)).astype(ml_dtypes.bfloat16)

    def cas(angle):
        return np.cos(angle) + np.sin(angle)

    quarter = np.arange(length // 4, dtype=np.int64)
    odd = 2 * quarter + 1
    whole = cas((quarter[:, None] * quarter[None, :] % (length // 4)) * (8.0 * math.pi / length))
    twice = cas((odd[:, None] * odd[None, :] % length) * (2.0 * math.pi / length))
    odd = 2 * np.arange(length // 2, dtype=np.int64) + 1
    half = cas((odd[:, None] * odd[None, :] % (2 * length)) * (math.pi / length))
    return parts(np.concatenate([whole, twice], axis=1)) + parts(half)


def pieces(block):
    high = block.astype(jnp.bfloat16)
    low = (block - high.astype(jnp.float32)).astype(jnp.bfloat16)
    return high, low


def product(a, b, dims):
    return lax.dot_general(a, b, (dims, ((), ())), preferred_element_type=jnp.float32)


def from_right(block, table_high, table_low):
    dims = ((1,), (0,))
    count = block.shape[0]
    if count <= TILE:
        high = block.astype(jnp.bfloat16).astype(jnp.float32)
        both = jnp.concatenate([high, block - high], axis=0).astype(jnp.bfloat16)
        main, rest = product(both, table_high, dims), product(both, table_low, dims)
        return main[:count] + main[count:] + rest[:count]
    high, low = pieces(block)
    return product(high, table_high, dims) + product(low, table_high, dims) + product(high, table_low, dims)


def transform(block, tables):
    quarter_high, quarter_low, half_high, half_low = tables
    half = half_high.shape[0]
    quarter = half // 2
    left, right = block[:, :half], block[:, half:]
    even, odd = left + right, left - right
    left, right = even[:, :quarter], even[:, quarter:]
    return jnp.concatenate([
        from_right(left + right, quarter_high[:, :quarter], quarter_low[:, :quarter]),
        from_right(left - right, quarter_high[:, quarter:], quarter_low[:, quarter:]),
        from_right(odd, half_high, half_low),
    ], axis=1)


def restore(block, tables):
    quarter_high, quarter_low, half_high, half_low = tables
    half = half_high.shape[0]
    quarter = half // 2
    left = from_right(block[:, :quarter], quarter_high[:, :quarter], quarter_low[:, :quarter])
    right = from_right(block[:, quarter:half], quarter_high[:, quarter:], quarter_low[:, quarter:])
    odd = from_right(block[:, half:], half_high, half_low)
    even = jnp.concatenate([left + right, left - right], axis=1)
    return jnp.concatenate([even + odd, even - odd], axis=1)


def read(tables):
    return [ref[...] for ref in tables]


def excess_of(levels):
    excess = jnp.full(levels.shape, -TIME_STEP * (DAMPING_TABLE[0] - MEAN_DAMPING), jnp.float32)
    for level_id in range(1, len(DAMPING_TABLE)):
        value = -TIME_STEP * (DAMPING_TABLE[level_id] - MEAN_DAMPING)
        excess = jnp.where(levels == level_id, value, excess)
    return excess


def roll(block, amount, axis):
    return pltpu.roll(block, amount % block.shape[axis], axis)


def waves(place, width):
    quarter, half = width // 4, width // 2
    even = jnp.where(place < quarter, 4 * place, 4 * (place - quarter) + 2)
    index = jnp.where(place < half, even, 2 * (place - half) + 1)
    return 4.0 * jnp.sin(index.astype(jnp.float32) * (math.pi / width)) ** 2


def own_terms(x, forcing, levels):
    excess = excess_of(levels)
    grad_cols = roll(x, -1, 1) - roll(x, 1, 1)
    terms = excess * x + TIME_STEP * forcing - (TIME_STEP / 8.0) * (grad_cols * grad_cols)
    return excess, terms


def start_all(pairs, sems):
    copies = [pltpu.make_async_copy(a, b, sems.at[i]) for i, (a, b) in enumerate(pairs)]
    for copy in copies:
        copy.start()
    return copies


def edge_kernel(step_ref, x_hbm, forcing_hbm, initial_hbm, levels_hbm, out_ref,
                x_ref, forcing_ref, initial_ref, levels_ref, sems):
    tile = x_ref.shape[0]
    last = pl.ds(x_hbm.shape[0] - tile, tile)
    copies = start_all([(x_hbm.at[last], x_ref), (forcing_hbm.at[last], forcing_ref),
                        (initial_hbm.at[last], initial_ref), (levels_hbm.at[last], levels_ref)], sems)
    for copy in copies:
        copy.wait()
    x = x_ref[...]
    _, terms = own_terms(x, forcing_ref[...], levels_ref[...])
    terms = terms + jnp.where(step_ref[0] == 0, initial_ref[...], 0.0)
    row = lax.broadcasted_iota(jnp.int32, x.shape, 0)
    out_ref[...] = jnp.where(row < tile // 2, roll(terms, tile // 2, 0), x)


def add_rows(x, last_step, source_ref):
    up, down = roll(x, 1, 0), roll(x, -1, 0)
    grad_rows = down - up
    source_ref[...] -= (TIME_STEP / 8.0) * (grad_rows * grad_rows)

    @pl.when(last_step)
    def _():
        lap = up + down + roll(x, 1, 1) + roll(x, -1, 1) - 4.0 * x
        lap_two = (
            roll(lap, 1, 0) + roll(lap, -1, 0) + roll(lap, 1, 1) + roll(lap, -1, 1) - 4.0 * lap
        )
        source_ref[...] -= x + TIME_STEP * (lap + lap_two + MEAN_DAMPING * x)


def load_kernel(steps, shift, step_ref, column_ref, x_hbm, forcing_hbm, initial_hbm, levels_hbm, *refs):
    count = (len(refs) - 10) // 2
    tables_hbm = refs[:count]
    x_ref, head_ref, ready_ref, excess_ref, gain_ref = refs[count : count + 5]
    tables = refs[count + 5 : 2 * count + 5]
    source_ref, forcing_ref, initial_ref, levels_ref, sems = refs[2 * count + 5 :]
    copies = start_all(
        [(x_hbm, x_ref), (levels_hbm, levels_ref), (forcing_hbm, forcing_ref)]
        + list(zip(tables_hbm, tables)), sems)
    late = pltpu.make_async_copy(initial_hbm, initial_ref, sems.at[len(copies)])

    @pl.when(step_ref[0] == 0)
    def _():
        late.start()

    shape = gain_ref.shape
    comps = shape[0] // 2
    lane = lax.broadcasted_iota(jnp.int32, shape, 1)
    row = lax.broadcasted_iota(jnp.int32, shape, 0)
    column = column_ref[0] + jnp.where(row >= comps, row - comps, row)
    modes = waves(lane, shape[1]) + waves(column, shape[1])
    gain_ref[...] = 1.0 / (1.0 + TIME_STEP * (modes * modes - modes + MEAN_DAMPING))
    for copy in copies[:3]:
        copy.wait()
    x = x_ref[...]
    excess, terms = own_terms(x, forcing_ref[...], levels_ref[...])
    excess_ref[...] = excess
    source_ref[...] = terms

    @pl.when(step_ref[0] == 0)
    def _():
        late.wait()
        source_ref[...] += initial_ref[...]

    head_ref[...] = source_ref[: head_ref.shape[0]]
    add_rows(x, step_ref[0] == steps - 1, source_ref)
    for copy in copies[3:]:
        copy.wait()
    ready_ref[...] = transform(roll(source_ref[...], shift, 0), read(tables)).T


def source_kernel(steps, shift, step_ref, x_ref, head_ref, ready_ref, edge_ref, *refs):
    tables, (out_ref, source_ref) = refs[:-2], refs[-2:]
    tile = edge_ref.shape[0]
    edge = edge_ref[...]
    x = jnp.concatenate([edge, x_ref[:tile]], axis=0)
    source_ref[...] = jnp.concatenate([roll(edge, tile // 2, 0), head_ref[...]], axis=0)
    add_rows(x, step_ref[0] == steps - 1, source_ref)
    first = transform(roll(source_ref[...], shift - tile, 0)[:tile], read(tables))
    out_ref[...] = ready_ref[...]
    out_ref[:, :tile] = first.T


def circulate(block, gain, steps):
    rows, lanes = block.shape
    powers = [gain]
    while len(powers) < steps.bit_length():
        powers.append(powers[-1] * powers[-1])
    start = gain / (1.0 - CIRCULANT_ALPHA * powers[-1])
    pack = gain.shape[0]
    half = pack // 2
    groups = rows // pack
    weight = jnp.where(
        lax.broadcasted_iota(jnp.int32, (pack, lanes), 0) < half, CIRCULANT_ALPHA, 1.0
    )
    u = [block[i * pack : (i + 1) * pack] * start for i in range(groups)]
    for j in range(steps.bit_length() - 1):
        k = 1 << j
        around = [weight * roll(part, half, 0) for part in u[groups - min(k, groups) :]]
        moved = around + u[: groups - len(around)]
        u = [part + powers[j] * other for part, other in zip(u, moved)]
    return jnp.concatenate(u, axis=0)


def solve_kernel(slabs, steps, shift, x_ref, gain_ref, *refs):
    tables, out_ref = read(refs[:-1]), refs[-1]
    rows = x_ref.shape[0] // slabs
    fields = jnp.concatenate([x_ref[pl.ds(s * rows, rows), :] for s in range(slabs)], axis=1)
    spectrum = transform(fields, tables)
    width = spectrum.shape[1]
    lanes = min(LANES, width)
    u = jnp.concatenate(
        [circulate(spectrum[:, i : i + lanes], gain_ref[:, i : i + lanes], steps)
         for i in range(0, width, lanes)], axis=1
    )
    result = restore(u, tables)
    if shift:
        result = roll(result, -shift, 1)
    for s in range(slabs):
        out_ref[pl.ds(s * rows, rows), :] = result[:, s * rows : (s + 1) * rows]


def sweep_kernel(steps, step_ref, y_ref, x_ref, excess_ref, *refs):
    tables, (out_ref, first_ref) = read(refs[:-2]), refs[-2:]
    keep = jnp.where(step_ref[0] == steps - 1, 0.0, 1.0)
    first = restore(y_ref[...].T, tables) - keep * x_ref[...]
    first_ref[...] = first
    out_ref[...] = transform(excess_ref[...] * first, tables).T


def finish_kernel(y_ref, first_ref, *refs):
    refs[-1][...] = restore(y_ref[...].T, read(refs[:-1])) + first_ref[...]


def call(kernel, out_shapes, specs, scratch=(), flops=0, bytes_accessed=0):
    return pl.pallas_call(
        kernel,
        out_shape=out_shapes,
        in_specs=specs,
        out_specs=[VMEM] * len(out_shapes) if isinstance(out_shapes, (list, tuple)) else VMEM,
        scratch_shapes=list(scratch),
        compiler_params=pltpu.CompilerParams(vmem_limit_bytes=16 * 1024 * 1024),
        cost_estimate=pl.CostEstimate(flops=flops, bytes_accessed=bytes_accessed, transcendentals=0),
    )


def local(iterate, forcing, initial, levels):
    field = iterate[0]
    rows, width = field.shape
    steps, slabs = lax.axis_size(TIME), lax.axis_size(SLAB)
    devices = steps * slabs
    comps = width // devices
    tables = [jnp.asarray(t) for t in hartley_tables(width)]
    step = lax.axis_index(TIME).astype(jnp.int32).reshape(1)
    column = (lax.axis_index(GROUP) * comps).astype(jnp.int32).reshape(1)
    plane = jax.ShapeDtypeStruct((rows, width), jnp.float32)
    turned = jax.ShapeDtypeStruct((width, rows), jnp.float32)
    strip = jax.ShapeDtypeStruct((TILE, width), jnp.float32)
    gains = jax.ShapeDtypeStruct((2 * comps, width), jnp.float32)
    work = 6 * 6 * rows * width * width // 16
    moved_bytes = 2 * width * width + 16 * rows * width

    def exchange(block):
        return lax.all_to_all(
            block.reshape(devices, comps, rows), GROUP, split_axis=0, concat_axis=0, tiled=True
        ).reshape(width, rows)

    stay = [pltpu.with_memory_space_constraint(a, pltpu.HBM)
            for a in (field, forcing[0], initial, levels)]
    stay_tables = [pltpu.with_memory_space_constraint(a, pltpu.HBM) for a in tables]
    buffers = [jnp.float32, jnp.float32, jnp.int32]

    edge = call(
        edge_kernel, strip, [SMEM] + [HBM] * 4,
        scratch=[pltpu.VMEM((TILE, width), kind) for kind in [jnp.float32] + buffers]
        + [pltpu.SemaphoreType.DMA((4,))],
        flops=32 * TILE * width, bytes_accessed=24 * TILE * width,
    )(step, *stay)
    edge = lax.ppermute(edge, SLAB, [(i, (i + 1) % slabs) for i in range(slabs)])
    field, head, ready, excess, gain, *tables = call(
        functools.partial(load_kernel, steps, SHIFT),
        [plane, strip, turned, plane, gains] + [jax.ShapeDtypeStruct(t.shape, t.dtype) for t in tables],
        [SMEM] * 2 + [HBM] * (4 + len(tables)),
        scratch=[pltpu.VMEM((rows, width), kind) for kind in [jnp.float32] + buffers]
        + [pltpu.SemaphoreType.DMA((4 + len(tables),))],
        flops=work, bytes_accessed=moved_bytes,
    )(step, column, *stay, *stay_tables)
    sent = call(
        functools.partial(source_kernel, steps, SHIFT), turned, [SMEM] + [VMEM] * (4 + len(tables)),
        scratch=[pltpu.VMEM((2 * TILE, width), jnp.float32)], flops=work, bytes_accessed=moved_bytes,
    )(step, field, head, ready, edge, *tables)

    def solve(block, shift):
        return exchange(call(
            functools.partial(solve_kernel, slabs, steps, shift), turned, [VMEM] * (2 + len(tables)),
            flops=2 * work, bytes_accessed=moved_bytes,
        )(exchange(block), gain, *tables))

    error, first = call(
        functools.partial(sweep_kernel, steps), [turned, plane], [SMEM] + [VMEM] * (3 + len(tables)),
        flops=2 * work, bytes_accessed=moved_bytes,
    )(step, solve(sent, SHIFT), field, excess, *tables)
    increment = call(
        finish_kernel, plane, [VMEM] * (2 + len(tables)), flops=work, bytes_accessed=moved_bytes
    )(solve(error, 0), first, *tables)
    return increment[None]


def solution(mesh):
    fine = jax.sharding.Mesh(mesh.devices.reshape(tuple(AXES.values())), tuple(AXES))
    placed = (P(TIME, SLAB, None), P(TIME, SLAB, None), P(SLAB, None), P(SLAB, None))
    return jax.shard_map(
        local, mesh=fine, in_specs=placed, out_specs=P(TIME, SLAB, None), check_vma=False
    )
```

```python
import functools
import math

import jax
import jax.numpy as jnp
import ml_dtypes
import numpy as np
from jax import lax
from jax.experimental import pallas as pl
from jax.experimental.pallas import tpu as pltpu
from jax.sharding import PartitionSpec as P

TIME_STEP = 0.05
CIRCULANT_ALPHA = 0.1
MEAN_DAMPING = 5.25
DAMPING_TABLE = (0.5, 1.0, 1.5, 2.5, 4.0, 6.0, 8.0, 10.0)
AXES = {"xh": 2, "z": 8, "c": 2, "xl": 2, "y": 4}
TIME = ("xh", "z", "c")
SLAB = ("xl", "y")
GROUP = ("xl", "y", "z", "c", "xh")
TILE = 8
LANES = 128
SHIFT = 2
VMEM = pl.BlockSpec(memory_space=pltpu.VMEM)
SMEM = pl.BlockSpec(memory_space=pltpu.SMEM)
HBM = pl.BlockSpec(memory_space=pltpu.HBM)


def hartley_tables(length, shift=0):
    def parts(table):
        table = table / math.sqrt(length)
        high = table.astype(ml_dtypes.bfloat16)
        return high, (table - high.astype(np.float64)).astype(ml_dtypes.bfloat16)

    def cas(angle):
        return np.cos(angle) + np.sin(angle)

    def moved(table, sign):
        return np.concatenate([table[:, shift:], sign * table[:, :shift]], axis=1)

    quarter = np.arange(length // 4, dtype=np.int64)
    odd = 2 * quarter + 1
    whole = cas((quarter[:, None] * quarter[None, :] % (length // 4)) * (8.0 * math.pi / length))
    twice = cas((odd[:, None] * odd[None, :] % length) * (2.0 * math.pi / length))
    odd = 2 * np.arange(length // 2, dtype=np.int64) + 1
    half = cas((odd[:, None] * odd[None, :] % (2 * length)) * (math.pi / length))
    return parts(np.concatenate([moved(whole, 1), moved(twice, -1)], axis=1)) + parts(moved(half, -1))


def pieces(block):
    high = block.astype(jnp.bfloat16)
    low = (block - high.astype(jnp.float32)).astype(jnp.bfloat16)
    return high, low


def product(a, b, dims):
    return lax.dot_general(a, b, (dims, ((), ())), preferred_element_type=jnp.float32)


def from_right(block, table_high, table_low):
    dims = ((1,), (0,))
    count = block.shape[0]
    if count <= TILE:
        high = block.astype(jnp.bfloat16).astype(jnp.float32)
        both = jnp.concatenate([high, block - high], axis=0).astype(jnp.bfloat16)
        main, rest = product(both, table_high, dims), product(both, table_low, dims)
        return main[:count] + main[count:] + rest[:count]
    high, low = pieces(block)
    return product(high, table_high, dims) + product(low, table_high, dims) + product(high, table_low, dims)


def transform(block, tables):
    quarter_high, quarter_low, half_high, half_low = tables
    half = half_high.shape[0]
    quarter = half // 2
    left, right = block[:, :half], block[:, half:]
    even, odd = left + right, left - right
    left, right = even[:, :quarter], even[:, quarter:]
    return jnp.concatenate([
        from_right(left + right, quarter_high[:, :quarter], quarter_low[:, :quarter]),
        from_right(left - right, quarter_high[:, quarter:], quarter_low[:, quarter:]),
        from_right(odd, half_high, half_low),
    ], axis=1)


def restore(block, tables):
    quarter_high, quarter_low, half_high, half_low = tables
    half = half_high.shape[0]
    quarter = half // 2
    left = from_right(block[:, :quarter], quarter_high[:, :quarter], quarter_low[:, :quarter])
    right = from_right(block[:, quarter:half], quarter_high[:, quarter:], quarter_low[:, quarter:])
    odd = from_right(block[:, half:], half_high, half_low)
    even = jnp.concatenate([left + right, left - right], axis=1)
    return jnp.concatenate([even + odd, even - odd], axis=1)


def read(tables):
    return [ref[...] for ref in tables]


def excess_of(levels):
    excess = jnp.full(levels.shape, -TIME_STEP * (DAMPING_TABLE[0] - MEAN_DAMPING), jnp.float32)
    for level_id in range(1, len(DAMPING_TABLE)):
        value = -TIME_STEP * (DAMPING_TABLE[level_id] - MEAN_DAMPING)
        excess = jnp.where(levels == level_id, value, excess)
    return excess


def roll(block, amount, axis):
    return pltpu.roll(block, amount % block.shape[axis], axis)


def waves(place, width):
    quarter, half = width // 4, width // 2
    even = jnp.where(place < quarter, 4 * place, 4 * (place - quarter) + 2)
    index = jnp.where(place < half, even, 2 * (place - half) + 1)
    return 4.0 * jnp.sin(index.astype(jnp.float32) * (math.pi / width)) ** 2


def own_terms(x, forcing, levels):
    excess = excess_of(levels)
    grad_cols = roll(x, -1, 1) - roll(x, 1, 1)
    terms = excess * x + TIME_STEP * forcing - (TIME_STEP / 8.0) * (grad_cols * grad_cols)
    return excess, terms


def start_all(pairs, sems):
    copies = [pltpu.make_async_copy(a, b, sems.at[i]) for i, (a, b) in enumerate(pairs)]
    for copy in copies:
        copy.start()
    return copies


def edge_kernel(step_ref, x_hbm, forcing_hbm, initial_hbm, levels_hbm, out_ref,
                x_ref, forcing_ref, initial_ref, levels_ref, sems):
    tile = x_ref.shape[0]
    last = pl.ds(x_hbm.shape[0] - tile, tile)
    copies = start_all([(x_hbm.at[last], x_ref), (forcing_hbm.at[last], forcing_ref),
                        (initial_hbm.at[last], initial_ref), (levels_hbm.at[last], levels_ref)], sems)
    for copy in copies:
        copy.wait()
    x = x_ref[...]
    _, terms = own_terms(x, forcing_ref[...], levels_ref[...])
    terms = terms + jnp.where(step_ref[0] == 0, initial_ref[...], 0.0)
    row = lax.broadcasted_iota(jnp.int32, x.shape, 0)
    out_ref[...] = jnp.where(row < tile // 2, roll(terms, tile // 2, 0), x)


def add_rows(x, last_step, source_ref):
    up, down = roll(x, 1, 0), roll(x, -1, 0)
    grad_rows = down - up
    source_ref[...] -= (TIME_STEP / 8.0) * (grad_rows * grad_rows)

    @pl.when(last_step)
    def _():
        lap = up + down + roll(x, 1, 1) + roll(x, -1, 1) - 4.0 * x
        lap_two = (
            roll(lap, 1, 0) + roll(lap, -1, 0) + roll(lap, 1, 1) + roll(lap, -1, 1) - 4.0 * lap
        )
        source_ref[...] -= x + TIME_STEP * (lap + lap_two + MEAN_DAMPING * x)


def load_kernel(steps, shift, step_ref, column_ref, x_hbm, forcing_hbm, initial_hbm, levels_hbm, *refs):
    count = (len(refs) - 10) // 2
    tables_hbm = refs[:count]
    x_ref, head_ref, ready_ref, excess_ref, gain_ref = refs[count : count + 5]
    tables = refs[count + 5 : 2 * count + 5]
    source_ref, forcing_ref, initial_ref, levels_ref, sems = refs[2 * count + 5 :]
    copies = start_all(
        [(x_hbm, x_ref), (levels_hbm, levels_ref), (forcing_hbm, forcing_ref)]
        + list(zip(tables_hbm, tables)), sems)
    late = pltpu.make_async_copy(initial_hbm, initial_ref, sems.at[len(copies)])

    @pl.when(step_ref[0] == 0)
    def _():
        late.start()

    shape = gain_ref.shape
    comps = shape[0] // 2
    lane = lax.broadcasted_iota(jnp.int32, shape, 1)
    row = lax.broadcasted_iota(jnp.int32, shape, 0)
    column = column_ref[0] + jnp.where(row >= comps, row - comps, row)
    modes = waves(lane, shape[1]) + waves(column, shape[1])
    gain_ref[...] = 1.0 / (1.0 + TIME_STEP * (modes * modes - modes + MEAN_DAMPING))
    for copy in copies[:3]:
        copy.wait()
    x = x_ref[...]
    excess, terms = own_terms(x, forcing_ref[...], levels_ref[...])
    excess_ref[...] = excess
    source_ref[...] = terms

    @pl.when(step_ref[0] == 0)
    def _():
        late.wait()
        source_ref[...] += initial_ref[...]

    head_ref[...] = source_ref[: head_ref.shape[0]]
    add_rows(x, step_ref[0] == steps - 1, source_ref)
    for copy in copies[3:]:
        copy.wait()
    ready_ref[...] = transform(roll(source_ref[...], shift, 0), read(tables)).T


def source_kernel(steps, shift, step_ref, x_ref, head_ref, ready_ref, edge_ref, *refs):
    tables, (out_ref, source_ref) = refs[:-2], refs[-2:]
    tile = edge_ref.shape[0]
    edge = edge_ref[...]
    x = jnp.concatenate([edge, x_ref[:tile]], axis=0)
    source_ref[...] = jnp.concatenate([roll(edge, tile // 2, 0), head_ref[...]], axis=0)
    add_rows(x, step_ref[0] == steps - 1, source_ref)
    first = transform(roll(source_ref[...], shift - tile, 0)[:tile], read(tables))
    out_ref[...] = ready_ref[...]
    out_ref[:, :tile] = first.T


def circulate(block, gain, steps):
    rows, lanes = block.shape
    powers = [gain]
    while len(powers) < steps.bit_length():
        powers.append(powers[-1] * powers[-1])
    start = gain / (1.0 - CIRCULANT_ALPHA * powers[-1])
    pack = gain.shape[0]
    half = pack // 2
    groups = rows // pack
    weight = jnp.where(
        lax.broadcasted_iota(jnp.int32, (pack, lanes), 0) < half, CIRCULANT_ALPHA, 1.0
    )
    u = [block[i * pack : (i + 1) * pack] * start for i in range(groups)]
    for j in range(steps.bit_length() - 1):
        k = 1 << j
        around = [weight * roll(part, half, 0) for part in u[groups - min(k, groups) :]]
        moved = around + u[: groups - len(around)]
        u = [part + powers[j] * other for part, other in zip(u, moved)]
    return jnp.concatenate(u, axis=0)


def solve_kernel(slabs, steps, x_ref, gain_ref, *refs):
    count = len(refs) // 2
    tables, inverse, out_ref = read(refs[:count]), read(refs[count:-1]), refs[-1]
    rows = x_ref.shape[0] // slabs
    fields = jnp.concatenate([x_ref[pl.ds(s * rows, rows), :] for s in range(slabs)], axis=1)
    spectrum = transform(fields, tables)
    width = spectrum.shape[1]
    lanes = min(LANES, width)
    u = jnp.concatenate(
        [circulate(spectrum[:, i : i + lanes], gain_ref[:, i : i + lanes], steps)
         for i in range(0, width, lanes)], axis=1
    )
    result = restore(u, inverse)
    for s in range(slabs):
        out_ref[pl.ds(s * rows, rows), :] = result[:, s * rows : (s + 1) * rows]


def sweep_kernel(steps, step_ref, y_ref, x_ref, excess_ref, *refs):
    tables, (out_ref, first_ref) = read(refs[:-2]), refs[-2:]
    keep = jnp.where(step_ref[0] == steps - 1, 0.0, 1.0)
    first = restore(y_ref[...].T, tables) - keep * x_ref[...]
    first_ref[...] = first
    out_ref[...] = transform(excess_ref[...] * first, tables).T


def finish_kernel(y_ref, first_ref, *refs):
    refs[-1][...] = restore(y_ref[...].T, read(refs[:-1])) + first_ref[...]


def call(kernel, out_shapes, specs, scratch=(), flops=0, bytes_accessed=0):
    return pl.pallas_call(
        kernel,
        out_shape=out_shapes,
        in_specs=specs,
        out_specs=[VMEM] * len(out_shapes) if isinstance(out_shapes, (list, tuple)) else VMEM,
        scratch_shapes=list(scratch),
        compiler_params=pltpu.CompilerParams(vmem_limit_bytes=16 * 1024 * 1024),
        cost_estimate=pl.CostEstimate(flops=flops, bytes_accessed=bytes_accessed, transcendentals=0),
    )


def local(iterate, forcing, initial, levels):
    field = iterate[0]
    rows, width = field.shape
    steps, slabs = lax.axis_size(TIME), lax.axis_size(SLAB)
    devices = steps * slabs
    comps = width // devices
    tables = [jnp.asarray(t) for t in hartley_tables(width)]
    shifted = [jnp.asarray(t) for t in hartley_tables(width, SHIFT)]
    step = lax.axis_index(TIME).astype(jnp.int32).reshape(1)
    column = (lax.axis_index(GROUP) * comps).astype(jnp.int32).reshape(1)
    plane = jax.ShapeDtypeStruct((rows, width), jnp.float32)
    turned = jax.ShapeDtypeStruct((width, rows), jnp.float32)
    strip = jax.ShapeDtypeStruct((TILE, width), jnp.float32)
    gains = jax.ShapeDtypeStruct((2 * comps, width), jnp.float32)
    work = 6 * 6 * rows * width * width // 16
    moved_bytes = 2 * width * width + 16 * rows * width

    def exchange(block):
        return lax.all_to_all(
            block.reshape(devices, comps, rows), GROUP, split_axis=0, concat_axis=0, tiled=True
        ).reshape(width, rows)

    stay = [pltpu.with_memory_space_constraint(a, pltpu.HBM)
            for a in (field, forcing[0], initial, levels)]
    stay_tables = [pltpu.with_memory_space_constraint(a, pltpu.HBM) for a in tables]
    buffers = [jnp.float32, jnp.float32, jnp.int32]

    edge = call(
        edge_kernel, strip, [SMEM] + [HBM] * 4,
        scratch=[pltpu.VMEM((TILE, width), kind) for kind in [jnp.float32] + buffers]
        + [pltpu.SemaphoreType.DMA((4,))],
        flops=32 * TILE * width, bytes_accessed=24 * TILE * width,
    )(step, *stay)
    edge = lax.ppermute(edge, SLAB, [(i, (i + 1) % slabs) for i in range(slabs)])
    field, head, ready, excess, gain, *tables = call(
        functools.partial(load_kernel, steps, SHIFT),
        [plane, strip, turned, plane, gains] + [jax.ShapeDtypeStruct(t.shape, t.dtype) for t in tables],
        [SMEM] * 2 + [HBM] * (4 + len(tables)),
        scratch=[pltpu.VMEM((rows, width), kind) for kind in [jnp.float32] + buffers]
        + [pltpu.SemaphoreType.DMA((4 + len(tables),))],
        flops=work, bytes_accessed=moved_bytes,
    )(step, column, *stay, *stay_tables)
    sent = call(
        functools.partial(source_kernel, steps, SHIFT), turned, [SMEM] + [VMEM] * (4 + len(tables)),
        scratch=[pltpu.VMEM((2 * TILE, width), jnp.float32)], flops=work, bytes_accessed=moved_bytes,
    )(step, field, head, ready, edge, *tables)

    def solve(block, inverse):
        return exchange(call(
            functools.partial(solve_kernel, slabs, steps), turned, [VMEM] * (2 + 2 * len(tables)),
            flops=2 * work, bytes_accessed=moved_bytes,
        )(exchange(block), gain, *tables, *inverse))

    error, first = call(
        functools.partial(sweep_kernel, steps), [turned, plane], [SMEM] + [VMEM] * (3 + len(tables)),
        flops=2 * work, bytes_accessed=moved_bytes,
    )(step, solve(sent, shifted), field, excess, *tables)
    increment = call(
        finish_kernel, plane, [VMEM] * (2 + len(tables)), flops=work, bytes_accessed=moved_bytes
    )(solve(error, tables), first, *tables)
    return increment[None]


def solution(mesh):
    fine = jax.sharding.Mesh(mesh.devices.reshape(tuple(AXES.values())), tuple(AXES))
    placed = (P(TIME, SLAB, None), P(TIME, SLAB, None), P(SLAB, None), P(SLAB, None))
    return jax.shard_map(
        local, mesh=fine, in_specs=placed, out_specs=P(TIME, SLAB, None), check_vma=False
    )
```

```python
import functools
import math

import jax
import jax.numpy as jnp
import ml_dtypes
import numpy as np
from jax import lax
from jax.experimental import pallas as pl
from jax.experimental.pallas import tpu as pltpu
from jax.sharding import PartitionSpec as P

TIME_STEP = 0.05
CIRCULANT_ALPHA = 0.1
MEAN_DAMPING = 5.25
DAMPING_TABLE = (0.5, 1.0, 1.5, 2.5, 4.0, 6.0, 8.0, 10.0)
AXES = {"xh": 2, "z": 8, "c": 2, "xl": 2, "y": 4}
TIME = ("xh", "z", "c")
SLAB = ("xl", "y")
GROUP = ("xl", "y", "z", "c", "xh")
TILE = 8
LANES = 128
SHIFT = 2
VMEM = pl.BlockSpec(memory_space=pltpu.VMEM)
SMEM = pl.BlockSpec(memory_space=pltpu.SMEM)
HBM = pl.BlockSpec(memory_space=pltpu.HBM)


def hartley_tables(length, shift=0):
    def parts(table):
        table = table / math.sqrt(length)
        high = table.astype(ml_dtypes.bfloat16)
        return high, (table - high.astype(np.float64)).astype(ml_dtypes.bfloat16)

    def cas(angle):
        return np.cos(angle) + np.sin(angle)

    def moved(table, sign):
        return np.concatenate([table[:, shift:], sign * table[:, :shift]], axis=1)

    quarter = np.arange(length // 4, dtype=np.int64)
    odd = 2 * quarter + 1
    whole = cas((quarter[:, None] * quarter[None, :] % (length // 4)) * (8.0 * math.pi / length))
    twice = cas((odd[:, None] * odd[None, :] % length) * (2.0 * math.pi / length))
    odd = 2 * np.arange(length // 2, dtype=np.int64) + 1
    half = cas((odd[:, None] * odd[None, :] % (2 * length)) * (math.pi / length))
    return parts(np.concatenate([moved(whole, 1), moved(twice, -1)], axis=1)) + parts(moved(half, -1))


def pieces(block):
    high = block.astype(jnp.bfloat16)
    low = (block - high.astype(jnp.float32)).astype(jnp.bfloat16)
    return high, low


def product(a, b, dims):
    return lax.dot_general(a, b, (dims, ((), ())), preferred_element_type=jnp.float32)


def from_right(block, table_high, table_low):
    dims = ((1,), (0,))
    count = block.shape[0]
    if count <= TILE:
        high = block.astype(jnp.bfloat16).astype(jnp.float32)
        both = jnp.concatenate([high, block - high], axis=0).astype(jnp.bfloat16)
        main, rest = product(both, table_high, dims), product(both, table_low, dims)
        return main[:count] + main[count:] + rest[:count]
    high, low = pieces(block)
    return product(high, table_high, dims) + product(low, table_high, dims) + product(high, table_low, dims)


def pieces_of(block, tables):
    quarter_high, quarter_low, half_high, half_low = tables
    half = half_high.shape[0]
    quarter = half // 2
    left, right = block[:, :half], block[:, half:]
    even, odd = left + right, left - right
    left, right = even[:, :quarter], even[:, quarter:]
    return [
        from_right(left + right, quarter_high[:, :quarter], quarter_low[:, :quarter]),
        from_right(left - right, quarter_high[:, quarter:], quarter_low[:, quarter:]),
        from_right(odd, half_high, half_low),
    ]


def transform(block, tables):
    return jnp.concatenate(pieces_of(block, tables), axis=1)


def transform_turned(block, tables, out_ref):
    start = 0
    for piece in pieces_of(block, tables):
        out_ref[start : start + piece.shape[1]] = piece.T
        start += piece.shape[1]


def joined(first, second, third, tables):
    quarter_high, quarter_low, half_high, half_low = tables
    quarter = half_high.shape[0] // 2
    left = from_right(first, quarter_high[:, :quarter], quarter_low[:, :quarter])
    right = from_right(second, quarter_high[:, quarter:], quarter_low[:, quarter:])
    odd = from_right(third, half_high, half_low)
    even = jnp.concatenate([left + right, left - right], axis=1)
    return jnp.concatenate([even + odd, even - odd], axis=1)


def restore(block, tables):
    half = tables[2].shape[0]
    return joined(block[:, : half // 2], block[:, half // 2 : half], block[:, half:], tables)


def restore_turned(ref, tables):
    half = tables[2].shape[0]
    return joined(ref[: half // 2].T, ref[half // 2 : half].T, ref[half:].T, tables)


def read(tables):
    return [ref[...] for ref in tables]


def excess_of(levels):
    excess = jnp.full(levels.shape, -TIME_STEP * (DAMPING_TABLE[0] - MEAN_DAMPING), jnp.float32)
    for level_id in range(1, len(DAMPING_TABLE)):
        value = -TIME_STEP * (DAMPING_TABLE[level_id] - MEAN_DAMPING)
        excess = jnp.where(levels == level_id, value, excess)
    return excess


def roll(block, amount, axis):
    return pltpu.roll(block, amount % block.shape[axis], axis)


def waves(place, width):
    quarter, half = width // 4, width // 2
    even = jnp.where(place < quarter, 4 * place, 4 * (place - quarter) + 2)
    index = jnp.where(place < half, even, 2 * (place - half) + 1)
    return 4.0 * jnp.sin(index.astype(jnp.float32) * (math.pi / width)) ** 2


def own_terms(x, forcing, levels):
    excess = excess_of(levels)
    grad_cols = roll(x, -1, 1) - roll(x, 1, 1)
    terms = excess * x + TIME_STEP * forcing - (TIME_STEP / 8.0) * (grad_cols * grad_cols)
    return excess, terms


def start_all(pairs, sems):
    copies = [pltpu.make_async_copy(a, b, sems.at[i]) for i, (a, b) in enumerate(pairs)]
    for copy in copies:
        copy.start()
    return copies


def edge_kernel(step_ref, x_hbm, forcing_hbm, initial_hbm, levels_hbm, out_ref,
                x_ref, forcing_ref, initial_ref, levels_ref, sems):
    tile = x_ref.shape[0]
    last = pl.ds(x_hbm.shape[0] - tile, tile)
    copies = start_all([(x_hbm.at[last], x_ref), (forcing_hbm.at[last], forcing_ref),
                        (initial_hbm.at[last], initial_ref), (levels_hbm.at[last], levels_ref)], sems)
    for copy in copies:
        copy.wait()
    x = x_ref[...]
    _, terms = own_terms(x, forcing_ref[...], levels_ref[...])
    terms = terms + jnp.where(step_ref[0] == 0, initial_ref[...], 0.0)
    row = lax.broadcasted_iota(jnp.int32, x.shape, 0)
    out_ref[...] = jnp.where(row < tile // 2, roll(terms, tile // 2, 0), x)


def add_rows(x, last_step, source_ref):
    up, down = roll(x, 1, 0), roll(x, -1, 0)
    grad_rows = down - up
    source_ref[...] -= (TIME_STEP / 8.0) * (grad_rows * grad_rows)

    @pl.when(last_step)
    def _():
        lap = up + down + roll(x, 1, 1) + roll(x, -1, 1) - 4.0 * x
        lap_two = (
            roll(lap, 1, 0) + roll(lap, -1, 0) + roll(lap, 1, 1) + roll(lap, -1, 1) - 4.0 * lap
        )
        source_ref[...] -= x + TIME_STEP * (lap + lap_two + MEAN_DAMPING * x)


def load_kernel(steps, shift, step_ref, column_ref, x_hbm, forcing_hbm, initial_hbm, levels_hbm, *refs):
    count = (len(refs) - 10) // 2
    tables_hbm = refs[:count]
    x_ref, head_ref, ready_ref, excess_ref, gain_ref = refs[count : count + 5]
    tables = refs[count + 5 : 2 * count + 5]
    source_ref, forcing_ref, initial_ref, levels_ref, sems = refs[2 * count + 5 :]
    copies = start_all(
        [(x_hbm, x_ref), (levels_hbm, levels_ref), (forcing_hbm, forcing_ref)]
        + list(zip(tables_hbm, tables)), sems)
    late = pltpu.make_async_copy(initial_hbm, initial_ref, sems.at[len(copies)])

    @pl.when(step_ref[0] == 0)
    def _():
        late.start()

    shape = gain_ref.shape
    comps = shape[0] // 2
    lane = lax.broadcasted_iota(jnp.int32, shape, 1)
    row = lax.broadcasted_iota(jnp.int32, shape, 0)
    column = column_ref[0] + jnp.where(row >= comps, row - comps, row)
    modes = waves(lane, shape[1]) + waves(column, shape[1])
    gain_ref[...] = 1.0 / (1.0 + TIME_STEP * (modes * modes - modes + MEAN_DAMPING))
    for copy in copies[:3]:
        copy.wait()
    x = x_ref[...]
    excess, terms = own_terms(x, forcing_ref[...], levels_ref[...])
    excess_ref[...] = excess
    source_ref[...] = terms

    @pl.when(step_ref[0] == 0)
    def _():
        late.wait()
        source_ref[...] += initial_ref[...]

    head_ref[...] = source_ref[: head_ref.shape[0]]
    add_rows(x, step_ref[0] == steps - 1, source_ref)
    for copy in copies[3:]:
        copy.wait()
    transform_turned(roll(source_ref[...], shift, 0), read(tables), ready_ref)


def source_kernel(steps, shift, step_ref, x_ref, head_ref, ready_ref, edge_ref, *refs):
    tables, (out_ref, source_ref) = refs[:-2], refs[-2:]
    tile = edge_ref.shape[0]
    edge = edge_ref[...]
    x = jnp.concatenate([edge, x_ref[:tile]], axis=0)
    source_ref[...] = jnp.concatenate([roll(edge, tile // 2, 0), head_ref[...]], axis=0)
    add_rows(x, step_ref[0] == steps - 1, source_ref)
    first = transform(roll(source_ref[...], shift - tile, 0)[:tile], read(tables))
    out_ref[...] = ready_ref[...]
    out_ref[:, :tile] = first.T


def circulate(block, gain, steps):
    rows, lanes = block.shape
    powers = [gain]
    while len(powers) < steps.bit_length():
        powers.append(powers[-1] * powers[-1])
    start = gain / (1.0 - CIRCULANT_ALPHA * powers[-1])
    pack = gain.shape[0]
    half = pack // 2
    groups = rows // pack
    weight = jnp.where(
        lax.broadcasted_iota(jnp.int32, (pack, lanes), 0) < half, CIRCULANT_ALPHA, 1.0
    )
    u = [block[i * pack : (i + 1) * pack] * start for i in range(groups)]
    for j in range(steps.bit_length() - 1):
        k = 1 << j
        around = [weight * roll(part, half, 0) for part in u[groups - min(k, groups) :]]
        moved = around + u[: groups - len(around)]
        u = [part + powers[j] * other for part, other in zip(u, moved)]
    return jnp.concatenate(u, axis=0)


def solve_kernel(slabs, steps, x_ref, gain_ref, *refs):
    count = len(refs) // 2
    tables, inverse, out_ref = read(refs[:count]), read(refs[count:-1]), refs[-1]
    rows = x_ref.shape[0] // slabs
    fields = jnp.concatenate([x_ref[pl.ds(s * rows, rows), :] for s in range(slabs)], axis=1)
    spectrum = transform(fields, tables)
    width = spectrum.shape[1]
    lanes = min(LANES, width)
    u = jnp.concatenate(
        [circulate(spectrum[:, i : i + lanes], gain_ref[:, i : i + lanes], steps)
         for i in range(0, width, lanes)], axis=1
    )
    result = restore(u, inverse)
    for s in range(slabs):
        out_ref[pl.ds(s * rows, rows), :] = result[:, s * rows : (s + 1) * rows]


def sweep_kernel(steps, step_ref, y_ref, x_ref, excess_ref, *refs):
    tables, (out_ref, first_ref) = read(refs[:-2]), refs[-2:]
    keep = jnp.where(step_ref[0] == steps - 1, 0.0, 1.0)
    first = restore_turned(y_ref, tables) - keep * x_ref[...]
    first_ref[...] = first
    transform_turned(excess_ref[...] * first, tables, out_ref)


def finish_kernel(y_ref, first_ref, *refs):
    refs[-1][...] = restore_turned(y_ref, read(refs[:-1])) + first_ref[...]


def call(kernel, out_shapes, specs, scratch=(), flops=0, bytes_accessed=0):
    return pl.pallas_call(
        kernel,
        out_shape=out_shapes,
        in_specs=specs,
        out_specs=[VMEM] * len(out_shapes) if isinstance(out_shapes, (list, tuple)) else VMEM,
        scratch_shapes=list(scratch),
        compiler_params=pltpu.CompilerParams(vmem_limit_bytes=16 * 1024 * 1024),
        cost_estimate=pl.CostEstimate(flops=flops, bytes_accessed=bytes_accessed, transcendentals=0),
    )


def local(iterate, forcing, initial, levels):
    field = iterate[0]
    rows, width = field.shape
    steps, slabs = lax.axis_size(TIME), lax.axis_size(SLAB)
    devices = steps * slabs
    comps = width // devices
    tables = [jnp.asarray(t) for t in hartley_tables(width)]
    shifted = [jnp.asarray(t) for t in hartley_tables(width, SHIFT)]
    step = lax.axis_index(TIME).astype(jnp.int32).reshape(1)
    column = (lax.axis_index(GROUP) * comps).astype(jnp.int32).reshape(1)
    plane = jax.ShapeDtypeStruct((rows, width), jnp.float32)
    turned = jax.ShapeDtypeStruct((width, rows), jnp.float32)
    strip = jax.ShapeDtypeStruct((TILE, width), jnp.float32)
    gains = jax.ShapeDtypeStruct((2 * comps, width), jnp.float32)
    work = 6 * 6 * rows * width * width // 16
    moved_bytes = 2 * width * width + 16 * rows * width

    def exchange(block):
        return lax.all_to_all(
            block.reshape(devices, comps, rows), GROUP, split_axis=0, concat_axis=0, tiled=True
        ).reshape(width, rows)

    stay = [pltpu.with_memory_space_constraint(a, pltpu.HBM)
            for a in (field, forcing[0], initial, levels)]
    stay_tables = [pltpu.with_memory_space_constraint(a, pltpu.HBM) for a in tables]
    buffers = [jnp.float32, jnp.float32, jnp.int32]

    edge = call(
        edge_kernel, strip, [SMEM] + [HBM] * 4,
        scratch=[pltpu.VMEM((TILE, width), kind) for kind in [jnp.float32] + buffers]
        + [pltpu.SemaphoreType.DMA((4,))],
        flops=32 * TILE * width, bytes_accessed=24 * TILE * width,
    )(step, *stay)
    edge = lax.ppermute(edge, SLAB, [(i, (i + 1) % slabs) for i in range(slabs)])
    field, head, ready, excess, gain, *tables = call(
        functools.partial(load_kernel, steps, SHIFT),
        [plane, strip, turned, plane, gains] + [jax.ShapeDtypeStruct(t.shape, t.dtype) for t in tables],
        [SMEM] * 2 + [HBM] * (4 + len(tables)),
        scratch=[pltpu.VMEM((rows, width), kind) for kind in [jnp.float32] + buffers]
        + [pltpu.SemaphoreType.DMA((4 + len(tables),))],
        flops=work, bytes_accessed=moved_bytes,
    )(step, column, *stay, *stay_tables)
    sent = call(
        functools.partial(source_kernel, steps, SHIFT), turned, [SMEM] + [VMEM] * (4 + len(tables)),
        scratch=[pltpu.VMEM((2 * TILE, width), jnp.float32)], flops=work, bytes_accessed=moved_bytes,
    )(step, field, head, ready, edge, *tables)

    def solve(block, inverse):
        return exchange(call(
            functools.partial(solve_kernel, slabs, steps), turned, [VMEM] * (2 + 2 * len(tables)),
            flops=2 * work, bytes_accessed=moved_bytes,
        )(exchange(block), gain, *tables, *inverse))

    error, first = call(
        functools.partial(sweep_kernel, steps), [turned, plane], [SMEM] + [VMEM] * (3 + len(tables)),
        flops=2 * work, bytes_accessed=moved_bytes,
    )(step, solve(sent, shifted), field, excess, *tables)
    increment = call(
        finish_kernel, plane, [VMEM] * (2 + len(tables)), flops=work, bytes_accessed=moved_bytes
    )(solve(error, tables), first, *tables)
    return increment[None]


def solution(mesh):
    fine = jax.sharding.Mesh(mesh.devices.reshape(tuple(AXES.values())), tuple(AXES))
    placed = (P(TIME, SLAB, None), P(TIME, SLAB, None), P(SLAB, None), P(SLAB, None))
    return jax.shard_map(
        local, mesh=fine, in_specs=placed, out_specs=P(TIME, SLAB, None), check_vma=False
    )
```

```python
import functools
import math

import jax
import jax.numpy as jnp
import ml_dtypes
import numpy as np
from jax import lax
from jax.experimental import pallas as pl
from jax.experimental.pallas import tpu as pltpu
from jax.sharding import PartitionSpec as P

TIME_STEP = 0.05
CIRCULANT_ALPHA = 0.1
MEAN_DAMPING = 5.25
DAMPING_TABLE = (0.5, 1.0, 1.5, 2.5, 4.0, 6.0, 8.0, 10.0)
AXES = {"xh": 2, "z": 8, "c": 2, "xl": 2, "y": 4}
TIME = ("xh", "z", "c")
SLAB = ("xl", "y")
GROUP = ("xl", "y", "z", "c", "xh")
TILE = 8
LANES = 256
SHIFT = 2
VMEM = pl.BlockSpec(memory_space=pltpu.VMEM)
SMEM = pl.BlockSpec(memory_space=pltpu.SMEM)
HBM = pl.BlockSpec(memory_space=pltpu.HBM)


def hartley_tables(length, shift=0):
    def parts(table):
        table = table / math.sqrt(length)
        high = table.astype(ml_dtypes.bfloat16)
        return high, (table - high.astype(np.float64)).astype(ml_dtypes.bfloat16)

    def cas(angle):
        return np.cos(angle) + np.sin(angle)

    def moved(table, sign):
        return np.concatenate([table[:, shift:], sign * table[:, :shift]], axis=1)

    quarter = np.arange(length // 4, dtype=np.int64)
    odd = 2 * quarter + 1
    whole = cas((quarter[:, None] * quarter[None, :] % (length // 4)) * (8.0 * math.pi / length))
    twice = cas((odd[:, None] * odd[None, :] % length) * (2.0 * math.pi / length))
    odd = 2 * np.arange(length // 2, dtype=np.int64) + 1
    half = cas((odd[:, None] * odd[None, :] % (2 * length)) * (math.pi / length))
    return parts(np.concatenate([moved(whole, 1), moved(twice, -1)], axis=1)) + parts(moved(half, -1))


def pieces(block):
    high = block.astype(jnp.bfloat16)
    low = (block - high.astype(jnp.float32)).astype(jnp.bfloat16)
    return high, low


def product(a, b, dims):
    return lax.dot_general(a, b, (dims, ((), ())), preferred_element_type=jnp.float32)


def from_right(block, table_high, table_low):
    dims = ((1,), (0,))
    count = block.shape[0]
    if count <= TILE:
        high = block.astype(jnp.bfloat16).astype(jnp.float32)
        both = jnp.concatenate([high, block - high], axis=0).astype(jnp.bfloat16)
        main, rest = product(both, table_high, dims), product(both, table_low, dims)
        return main[:count] + main[count:] + rest[:count]
    high, low = pieces(block)
    return product(high, table_high, dims) + product(low, table_high, dims) + product(high, table_low, dims)


def transform(block, tables):
    quarter_high, quarter_low, half_high, half_low = tables
    half = half_high.shape[0]
    quarter = half // 2
    left, right = block[:, :half], block[:, half:]
    even, odd = left + right, left - right
    left, right = even[:, :quarter], even[:, quarter:]
    return jnp.concatenate([
        from_right(left + right, quarter_high[:, :quarter], quarter_low[:, :quarter]),
        from_right(left - right, quarter_high[:, quarter:], quarter_low[:, quarter:]),
        from_right(odd, half_high, half_low),
    ], axis=1)


def restore(block, tables):
    quarter_high, quarter_low, half_high, half_low = tables
    half = half_high.shape[0]
    quarter = half // 2
    left = from_right(block[:, :quarter], quarter_high[:, :quarter], quarter_low[:, :quarter])
    right = from_right(block[:, quarter:half], quarter_high[:, quarter:], quarter_low[:, quarter:])
    odd = from_right(block[:, half:], half_high, half_low)
    even = jnp.concatenate([left + right, left - right], axis=1)
    return jnp.concatenate([even + odd, even - odd], axis=1)


def read(tables):
    return [ref[...] for ref in tables]


def excess_of(levels):
    excess = jnp.full(levels.shape, -TIME_STEP * (DAMPING_TABLE[0] - MEAN_DAMPING), jnp.float32)
    for level_id in range(1, len(DAMPING_TABLE)):
        value = -TIME_STEP * (DAMPING_TABLE[level_id] - MEAN_DAMPING)
        excess = jnp.where(levels == level_id, value, excess)
    return excess


def roll(block, amount, axis):
    return pltpu.roll(block, amount % block.shape[axis], axis)


def waves(place, width):
    quarter, half = width // 4, width // 2
    even = jnp.where(place < quarter, 4 * place, 4 * (place - quarter) + 2)
    index = jnp.where(place < half, even, 2 * (place - half) + 1)
    return 4.0 * jnp.sin(index.astype(jnp.float32) * (math.pi / width)) ** 2


def own_terms(x, forcing, levels):
    excess = excess_of(levels)
    grad_cols = roll(x, -1, 1) - roll(x, 1, 1)
    terms = excess * x + TIME_STEP * forcing - (TIME_STEP / 8.0) * (grad_cols * grad_cols)
    return excess, terms


def start_all(pairs, sems):
    copies = [pltpu.make_async_copy(a, b, sems.at[i]) for i, (a, b) in enumerate(pairs)]
    for copy in copies:
        copy.start()
    return copies


def edge_kernel(step_ref, x_hbm, forcing_hbm, initial_hbm, levels_hbm, out_ref,
                x_ref, forcing_ref, initial_ref, levels_ref, sems):
    tile = x_ref.shape[0]
    last = pl.ds(x_hbm.shape[0] - tile, tile)
    copies = start_all([(x_hbm.at[last], x_ref), (forcing_hbm.at[last], forcing_ref),
                        (initial_hbm.at[last], initial_ref), (levels_hbm.at[last], levels_ref)], sems)
    for copy in copies:
        copy.wait()
    x = x_ref[...]
    _, terms = own_terms(x, forcing_ref[...], levels_ref[...])
    terms = terms + jnp.where(step_ref[0] == 0, initial_ref[...], 0.0)
    row = lax.broadcasted_iota(jnp.int32, x.shape, 0)
    out_ref[...] = jnp.where(row < tile // 2, roll(terms, tile // 2, 0), x)


def add_rows(x, last_step, source_ref):
    up, down = roll(x, 1, 0), roll(x, -1, 0)
    grad_rows = down - up
    source_ref[...] -= (TIME_STEP / 8.0) * (grad_rows * grad_rows)

    @pl.when(last_step)
    def _():
        lap = up + down + roll(x, 1, 1) + roll(x, -1, 1) - 4.0 * x
        lap_two = (
            roll(lap, 1, 0) + roll(lap, -1, 0) + roll(lap, 1, 1) + roll(lap, -1, 1) - 4.0 * lap
        )
        source_ref[...] -= x + TIME_STEP * (lap + lap_two + MEAN_DAMPING * x)


def load_kernel(steps, shift, step_ref, column_ref, x_hbm, forcing_hbm, initial_hbm, levels_hbm, *refs):
    count = (len(refs) - 10) // 2
    tables_hbm = refs[:count]
    x_ref, head_ref, ready_ref, excess_ref, gain_ref = refs[count : count + 5]
    tables = refs[count + 5 : 2 * count + 5]
    source_ref, forcing_ref, initial_ref, levels_ref, sems = refs[2 * count + 5 :]
    copies = start_all(
        [(x_hbm, x_ref), (levels_hbm, levels_ref), (forcing_hbm, forcing_ref)]
        + list(zip(tables_hbm, tables)), sems)
    late = pltpu.make_async_copy(initial_hbm, initial_ref, sems.at[len(copies)])

    @pl.when(step_ref[0] == 0)
    def _():
        late.start()

    shape = gain_ref.shape
    comps = shape[0] // 2
    lane = lax.broadcasted_iota(jnp.int32, shape, 1)
    row = lax.broadcasted_iota(jnp.int32, shape, 0)
    column = column_ref[0] + jnp.where(row >= comps, row - comps, row)
    modes = waves(lane, shape[1]) + waves(column, shape[1])
    gain_ref[...] = 1.0 / (1.0 + TIME_STEP * (modes * modes - modes + MEAN_DAMPING))
    for copy in copies[:3]:
        copy.wait()
    x = x_ref[...]
    excess, terms = own_terms(x, forcing_ref[...], levels_ref[...])
    excess_ref[...] = excess
    source_ref[...] = terms

    @pl.when(step_ref[0] == 0)
    def _():
        late.wait()
        source_ref[...] += initial_ref[...]

    head_ref[...] = source_ref[: head_ref.shape[0]]
    add_rows(x, step_ref[0] == steps - 1, source_ref)
    for copy in copies[3:]:
        copy.wait()
    ready_ref[...] = transform(roll(source_ref[...], shift, 0), read(tables)).T


def source_kernel(steps, shift, step_ref, x_ref, head_ref, ready_ref, edge_ref, *refs):
    tables, (out_ref, source_ref) = refs[:-2], refs[-2:]
    tile = edge_ref.shape[0]
    edge = edge_ref[...]
    x = jnp.concatenate([edge, x_ref[:tile]], axis=0)
    source_ref[...] = jnp.concatenate([roll(edge, tile // 2, 0), head_ref[...]], axis=0)
    add_rows(x, step_ref[0] == steps - 1, source_ref)
    first = transform(roll(source_ref[...], shift - tile, 0)[:tile], read(tables))
    out_ref[...] = ready_ref[...]
    out_ref[:, :tile] = first.T


def circulate(block, gain, steps):
    rows, lanes = block.shape
    powers = [gain]
    while len(powers) < steps.bit_length():
        powers.append(powers[-1] * powers[-1])
    start = gain / (1.0 - CIRCULANT_ALPHA * powers[-1])
    pack = gain.shape[0]
    half = pack // 2
    groups = rows // pack
    weight = jnp.where(
        lax.broadcasted_iota(jnp.int32, (pack, lanes), 0) < half, CIRCULANT_ALPHA, 1.0
    )
    u = [block[i * pack : (i + 1) * pack] * start for i in range(groups)]
    for j in range(steps.bit_length() - 1):
        k = 1 << j
        around = [weight * roll(part, half, 0) for part in u[groups - min(k, groups) :]]
        moved = around + u[: groups - len(around)]
        u = [part + powers[j] * other for part, other in zip(u, moved)]
    return jnp.concatenate(u, axis=0)


def solve_kernel(slabs, steps, x_ref, gain_ref, *refs):
    count = len(refs) // 2
    tables, inverse, out_ref = read(refs[:count]), read(refs[count:-1]), refs[-1]
    rows = x_ref.shape[0] // slabs
    fields = jnp.concatenate([x_ref[pl.ds(s * rows, rows), :] for s in range(slabs)], axis=1)
    spectrum = transform(fields, tables)
    width = spectrum.shape[1]
    lanes = min(LANES, width)
    u = jnp.concatenate(
        [circulate(spectrum[:, i : i + lanes], gain_ref[:, i : i + lanes], steps)
         for i in range(0, width, lanes)], axis=1
    )
    result = restore(u, inverse)
    for s in range(slabs):
        out_ref[pl.ds(s * rows, rows), :] = result[:, s * rows : (s + 1) * rows]


def sweep_kernel(steps, step_ref, y_ref, x_ref, excess_ref, *refs):
    tables, (out_ref, first_ref) = read(refs[:-2]), refs[-2:]
    keep = jnp.where(step_ref[0] == steps - 1, 0.0, 1.0)
    first = restore(y_ref[...].T, tables) - keep * x_ref[...]
    first_ref[...] = first
    out_ref[...] = transform(excess_ref[...] * first, tables).T


def finish_kernel(y_ref, first_ref, *refs):
    refs[-1][...] = restore(y_ref[...].T, read(refs[:-1])) + first_ref[...]


def call(kernel, out_shapes, specs, scratch=(), flops=0, bytes_accessed=0):
    return pl.pallas_call(
        kernel,
        out_shape=out_shapes,
        in_specs=specs,
        out_specs=[VMEM] * len(out_shapes) if isinstance(out_shapes, (list, tuple)) else VMEM,
        scratch_shapes=list(scratch),
        compiler_params=pltpu.CompilerParams(vmem_limit_bytes=16 * 1024 * 1024),
        cost_estimate=pl.CostEstimate(flops=flops, bytes_accessed=bytes_accessed, transcendentals=0),
    )


def local(iterate, forcing, initial, levels):
    field = iterate[0]
    rows, width = field.shape
    steps, slabs = lax.axis_size(TIME), lax.axis_size(SLAB)
    devices = steps * slabs
    comps = width // devices
    tables = [jnp.asarray(t) for t in hartley_tables(width)]
    shifted = [jnp.asarray(t) for t in hartley_tables(width, SHIFT)]
    step = lax.axis_index(TIME).astype(jnp.int32).reshape(1)
    column = (lax.axis_index(GROUP) * comps).astype(jnp.int32).reshape(1)
    plane = jax.ShapeDtypeStruct((rows, width), jnp.float32)
    turned = jax.ShapeDtypeStruct((width, rows), jnp.float32)
    strip = jax.ShapeDtypeStruct((TILE, width), jnp.float32)
    gains = jax.ShapeDtypeStruct((2 * comps, width), jnp.float32)
    work = 6 * 6 * rows * width * width // 16
    moved_bytes = 2 * width * width + 16 * rows * width

    def exchange(block):
        return lax.all_to_all(
            block.reshape(devices, comps, rows), GROUP, split_axis=0, concat_axis=0, tiled=True
        ).reshape(width, rows)

    stay = [pltpu.with_memory_space_constraint(a, pltpu.HBM)
            for a in (field, forcing[0], initial, levels)]
    stay_tables = [pltpu.with_memory_space_constraint(a, pltpu.HBM) for a in tables]
    buffers = [jnp.float32, jnp.float32, jnp.int32]

    edge = call(
        edge_kernel, strip, [SMEM] + [HBM] * 4,
        scratch=[pltpu.VMEM((TILE, width), kind) for kind in [jnp.float32] + buffers]
        + [pltpu.SemaphoreType.DMA((4,))],
        flops=32 * TILE * width, bytes_accessed=24 * TILE * width,
    )(step, *stay)
    edge = lax.ppermute(edge, SLAB, [(i, (i + 1) % slabs) for i in range(slabs)])
    field, head, ready, excess, gain, *tables = call(
        functools.partial(load_kernel, steps, SHIFT),
        [plane, strip, turned, plane, gains] + [jax.ShapeDtypeStruct(t.shape, t.dtype) for t in tables],
        [SMEM] * 2 + [HBM] * (4 + len(tables)),
        scratch=[pltpu.VMEM((rows, width), kind) for kind in [jnp.float32] + buffers]
        + [pltpu.SemaphoreType.DMA((4 + len(tables),))],
        flops=work, bytes_accessed=moved_bytes,
    )(step, column, *stay, *stay_tables)
    sent = call(
        functools.partial(source_kernel, steps, SHIFT), turned, [SMEM] + [VMEM] * (4 + len(tables)),
        scratch=[pltpu.VMEM((2 * TILE, width), jnp.float32)], flops=work, bytes_accessed=moved_bytes,
    )(step, field, head, ready, edge, *tables)

    def solve(block, inverse):
        return exchange(call(
            functools.partial(solve_kernel, slabs, steps), turned, [VMEM] * (2 + 2 * len(tables)),
            flops=2 * work, bytes_accessed=moved_bytes,
        )(exchange(block), gain, *tables, *inverse))

    error, first = call(
        functools.partial(sweep_kernel, steps), [turned, plane], [SMEM] + [VMEM] * (3 + len(tables)),
        flops=2 * work, bytes_accessed=moved_bytes,
    )(step, solve(sent, shifted), field, excess, *tables)
    increment = call(
        finish_kernel, plane, [VMEM] * (2 + len(tables)), flops=work, bytes_accessed=moved_bytes
    )(solve(error, tables), first, *tables)
    return increment[None]


def solution(mesh):
    fine = jax.sharding.Mesh(mesh.devices.reshape(tuple(AXES.values())), tuple(AXES))
    placed = (P(TIME, SLAB, None), P(TIME, SLAB, None), P(SLAB, None), P(SLAB, None))
    return jax.shard_map(
        local, mesh=fine, in_specs=placed, out_specs=P(TIME, SLAB, None), check_vma=False
    )
```

```python
import functools
import math

import jax
import jax.numpy as jnp
import ml_dtypes
import numpy as np
from jax import lax
from jax.experimental import pallas as pl
from jax.experimental.pallas import tpu as pltpu
from jax.sharding import PartitionSpec as P

TIME_STEP = 0.05
CIRCULANT_ALPHA = 0.1
MEAN_DAMPING = 5.25
DAMPING_TABLE = (0.5, 1.0, 1.5, 2.5, 4.0, 6.0, 8.0, 10.0)
AXES = {"xh": 2, "z": 8, "c": 2, "xl": 2, "y": 4}
TIME = ("xh", "z", "c")
SLAB = ("xl", "y")
GROUP = ("xl", "y", "z", "c", "xh")
TILE = 8
LANES = 128
SHIFT = 2
VMEM = pl.BlockSpec(memory_space=pltpu.VMEM)
SMEM = pl.BlockSpec(memory_space=pltpu.SMEM)
HBM = pl.BlockSpec(memory_space=pltpu.HBM)


def hartley_tables(length, shift=0):
    def parts(table):
        table = table / math.sqrt(length)
        high = table.astype(ml_dtypes.bfloat16)
        return high, (table - high.astype(np.float64)).astype(ml_dtypes.bfloat16)

    def cas(angle):
        return np.cos(angle) + np.sin(angle)

    def moved(table, sign):
        return np.concatenate([table[:, shift:], sign * table[:, :shift]], axis=1)

    quarter = np.arange(length // 4, dtype=np.int64)
    odd = 2 * quarter + 1
    whole = cas((quarter[:, None] * quarter[None, :] % (length // 4)) * (8.0 * math.pi / length))
    twice = cas((odd[:, None] * odd[None, :] % length) * (2.0 * math.pi / length))
    odd = 2 * np.arange(length // 2, dtype=np.int64) + 1
    half = cas((odd[:, None] * odd[None, :] % (2 * length)) * (math.pi / length))
    return parts(np.concatenate([moved(whole, 1), moved(twice, -1)], axis=1)) + parts(moved(half, -1))


def pieces(block):
    high = block.astype(jnp.bfloat16)
    low = (block - high.astype(jnp.float32)).astype(jnp.bfloat16)
    return high, low


def product(a, b, dims):
    return lax.dot_general(a, b, (dims, ((), ())), preferred_element_type=jnp.float32)


def from_right(block, table_high, table_low, stacked=False):
    dims = ((1,), (0,))
    count = block.shape[0]
    if stacked or count <= TILE:
        high = block.astype(jnp.bfloat16).astype(jnp.float32)
        both = jnp.concatenate([high, block - high], axis=0).astype(jnp.bfloat16)
        main, rest = product(both, table_high, dims), product(both[: max(count, 2 * TILE)], table_low, dims)
        return main[:count] + main[count:] + rest[:count]
    high, low = pieces(block)
    return product(high, table_high, dims) + product(low, table_high, dims) + product(high, table_low, dims)


def transform(block, tables, stacked=False):
    quarter_high, quarter_low, half_high, half_low = tables
    half = half_high.shape[0]
    quarter = half // 2
    left, right = block[:, :half], block[:, half:]
    even, odd = left + right, left - right
    left, right = even[:, :quarter], even[:, quarter:]
    return jnp.concatenate([
        from_right(left + right, quarter_high[:, :quarter], quarter_low[:, :quarter], stacked),
        from_right(left - right, quarter_high[:, quarter:], quarter_low[:, quarter:], stacked),
        from_right(odd, half_high, half_low, stacked),
    ], axis=1)


def restore(block, tables):
    quarter_high, quarter_low, half_high, half_low = tables
    half = half_high.shape[0]
    quarter = half // 2
    left = from_right(block[:, :quarter], quarter_high[:, :quarter], quarter_low[:, :quarter])
    right = from_right(block[:, quarter:half], quarter_high[:, quarter:], quarter_low[:, quarter:])
    odd = from_right(block[:, half:], half_high, half_low)
    even = jnp.concatenate([left + right, left - right], axis=1)
    return jnp.concatenate([even + odd, even - odd], axis=1)


def read(tables):
    return [ref[...] for ref in tables]


def excess_of(levels):
    excess = jnp.full(levels.shape, -TIME_STEP * (DAMPING_TABLE[0] - MEAN_DAMPING), jnp.float32)
    for level_id in range(1, len(DAMPING_TABLE)):
        value = -TIME_STEP * (DAMPING_TABLE[level_id] - MEAN_DAMPING)
        excess = jnp.where(levels == level_id, value, excess)
    return excess


def roll(block, amount, axis):
    return pltpu.roll(block, amount % block.shape[axis], axis)


def waves(place, width):
    quarter, half = width // 4, width // 2
    even = jnp.where(place < quarter, 4 * place, 4 * (place - quarter) + 2)
    index = jnp.where(place < half, even, 2 * (place - half) + 1)
    return 4.0 * jnp.sin(index.astype(jnp.float32) * (math.pi / width)) ** 2


def own_terms(x, forcing, levels):
    excess = excess_of(levels)
    grad_cols = roll(x, -1, 1) - roll(x, 1, 1)
    terms = excess * x + TIME_STEP * forcing - (TIME_STEP / 8.0) * (grad_cols * grad_cols)
    return excess, terms


def start_all(pairs, sems):
    copies = [pltpu.make_async_copy(a, b, sems.at[i]) for i, (a, b) in enumerate(pairs)]
    for copy in copies:
        copy.start()
    return copies


def edge_kernel(step_ref, x_hbm, forcing_hbm, initial_hbm, levels_hbm, out_ref,
                x_ref, forcing_ref, initial_ref, levels_ref, sems):
    tile = x_ref.shape[0]
    last = pl.ds(x_hbm.shape[0] - tile, tile)
    copies = start_all([(x_hbm.at[last], x_ref), (forcing_hbm.at[last], forcing_ref),
                        (initial_hbm.at[last], initial_ref), (levels_hbm.at[last], levels_ref)], sems)
    for copy in copies:
        copy.wait()
    x = x_ref[...]
    _, terms = own_terms(x, forcing_ref[...], levels_ref[...])
    terms = terms + jnp.where(step_ref[0] == 0, initial_ref[...], 0.0)
    row = lax.broadcasted_iota(jnp.int32, x.shape, 0)
    out_ref[...] = jnp.where(row < tile // 2, roll(terms, tile // 2, 0), x)


def add_rows(x, last_step, source_ref):
    up, down = roll(x, 1, 0), roll(x, -1, 0)
    grad_rows = down - up
    source_ref[...] -= (TIME_STEP / 8.0) * (grad_rows * grad_rows)

    @pl.when(last_step)
    def _():
        lap = up + down + roll(x, 1, 1) + roll(x, -1, 1) - 4.0 * x
        lap_two = (
            roll(lap, 1, 0) + roll(lap, -1, 0) + roll(lap, 1, 1) + roll(lap, -1, 1) - 4.0 * lap
        )
        source_ref[...] -= x + TIME_STEP * (lap + lap_two + MEAN_DAMPING * x)


def load_kernel(steps, shift, step_ref, column_ref, x_hbm, forcing_hbm, initial_hbm, levels_hbm, *refs):
    count = (len(refs) - 10) // 2
    tables_hbm = refs[:count]
    x_ref, head_ref, ready_ref, excess_ref, gain_ref = refs[count : count + 5]
    tables = refs[count + 5 : 2 * count + 5]
    source_ref, forcing_ref, initial_ref, levels_ref, sems = refs[2 * count + 5 :]
    copies = start_all(
        [(x_hbm, x_ref), (levels_hbm, levels_ref), (forcing_hbm, forcing_ref)]
        + list(zip(tables_hbm, tables)), sems)
    late = pltpu.make_async_copy(initial_hbm, initial_ref, sems.at[len(copies)])

    @pl.when(step_ref[0] == 0)
    def _():
        late.start()

    shape = gain_ref.shape
    comps = shape[0] // 2
    lane = lax.broadcasted_iota(jnp.int32, shape, 1)
    row = lax.broadcasted_iota(jnp.int32, shape, 0)
    column = column_ref[0] + jnp.where(row >= comps, row - comps, row)
    modes = waves(lane, shape[1]) + waves(column, shape[1])
    gain_ref[...] = 1.0 / (1.0 + TIME_STEP * (modes * modes - modes + MEAN_DAMPING))
    for copy in copies[:3]:
        copy.wait()
    x = x_ref[...]
    excess, terms = own_terms(x, forcing_ref[...], levels_ref[...])
    excess_ref[...] = excess
    source_ref[...] = terms

    @pl.when(step_ref[0] == 0)
    def _():
        late.wait()
        source_ref[...] += initial_ref[...]

    head_ref[...] = source_ref[: head_ref.shape[0]]
    add_rows(x, step_ref[0] == steps - 1, source_ref)
    for copy in copies[3:]:
        copy.wait()
    ready_ref[...] = transform(roll(source_ref[...], shift, 0), read(tables)).T


def source_kernel(steps, shift, step_ref, x_ref, head_ref, ready_ref, edge_ref, *refs):
    tables, (out_ref, source_ref) = refs[:-2], refs[-2:]
    tile = edge_ref.shape[0]
    edge = edge_ref[...]
    x = jnp.concatenate([edge, x_ref[:tile]], axis=0)
    source_ref[...] = jnp.concatenate([roll(edge, tile // 2, 0), head_ref[...]], axis=0)
    add_rows(x, step_ref[0] == steps - 1, source_ref)
    first = transform(roll(source_ref[...], shift - tile, 0)[:tile], read(tables))
    out_ref[...] = ready_ref[...]
    out_ref[:, :tile] = first.T


def circulate(block, gain, steps):
    rows, lanes = block.shape
    powers = [gain]
    while len(powers) < steps.bit_length():
        powers.append(powers[-1] * powers[-1])
    start = gain / (1.0 - CIRCULANT_ALPHA * powers[-1])
    pack = gain.shape[0]
    half = pack // 2
    groups = rows // pack
    weight = jnp.where(
        lax.broadcasted_iota(jnp.int32, (pack, lanes), 0) < half, CIRCULANT_ALPHA, 1.0
    )
    u = [block[i * pack : (i + 1) * pack] * start for i in range(groups)]
    for j in range(steps.bit_length() - 1):
        k = 1 << j
        around = [weight * roll(part, half, 0) for part in u[groups - min(k, groups) :]]
        moved = around + u[: groups - len(around)]
        u = [part + powers[j] * other for part, other in zip(u, moved)]
    return jnp.concatenate(u, axis=0)


def solve_kernel(slabs, steps, x_ref, gain_ref, *refs):
    count = len(refs) // 2
    tables, inverse, out_ref = read(refs[:count]), read(refs[count:-1]), refs[-1]
    rows = x_ref.shape[0] // slabs
    fields = jnp.concatenate([x_ref[pl.ds(s * rows, rows), :] for s in range(slabs)], axis=1)
    spectrum = transform(fields, tables)
    width = spectrum.shape[1]
    lanes = min(LANES, width)
    u = jnp.concatenate(
        [circulate(spectrum[:, i : i + lanes], gain_ref[:, i : i + lanes], steps)
         for i in range(0, width, lanes)], axis=1
    )
    result = restore(u, inverse)
    for s in range(slabs):
        out_ref[pl.ds(s * rows, rows), :] = result[:, s * rows : (s + 1) * rows]


def sweep_kernel(steps, step_ref, y_ref, x_ref, excess_ref, *refs):
    tables, (out_ref, first_ref) = read(refs[:-2]), refs[-2:]
    keep = jnp.where(step_ref[0] == steps - 1, 0.0, 1.0)
    first = restore(y_ref[...].T, tables) - keep * x_ref[...]
    first_ref[...] = first
    out_ref[...] = transform(excess_ref[...] * first, tables, True).T


def finish_kernel(y_ref, first_ref, *refs):
    refs[-1][...] = restore(y_ref[...].T, read(refs[:-1])) + first_ref[...]


def call(kernel, out_shapes, specs, scratch=(), flops=0, bytes_accessed=0):
    return pl.pallas_call(
        kernel,
        out_shape=out_shapes,
        in_specs=specs,
        out_specs=[VMEM] * len(out_shapes) if isinstance(out_shapes, (list, tuple)) else VMEM,
        scratch_shapes=list(scratch),
        compiler_params=pltpu.CompilerParams(vmem_limit_bytes=16 * 1024 * 1024),
        cost_estimate=pl.CostEstimate(flops=flops, bytes_accessed=bytes_accessed, transcendentals=0),
    )


def local(iterate, forcing, initial, levels):
    field = iterate[0]
    rows, width = field.shape
    steps, slabs = lax.axis_size(TIME), lax.axis_size(SLAB)
    devices = steps * slabs
    comps = width // devices
    tables = [jnp.asarray(t) for t in hartley_tables(width)]
    shifted = [jnp.asarray(t) for t in hartley_tables(width, SHIFT)]
    step = lax.axis_index(TIME).astype(jnp.int32).reshape(1)
    column = (lax.axis_index(GROUP) * comps).astype(jnp.int32).reshape(1)
    plane = jax.ShapeDtypeStruct((rows, width), jnp.float32)
    turned = jax.ShapeDtypeStruct((width, rows), jnp.float32)
    strip = jax.ShapeDtypeStruct((TILE, width), jnp.float32)
    gains = jax.ShapeDtypeStruct((2 * comps, width), jnp.float32)
    work = 6 * 6 * rows * width * width // 16
    moved_bytes = 2 * width * width + 16 * rows * width

    def exchange(block):
        return lax.all_to_all(
            block.reshape(devices, comps, rows), GROUP, split_axis=0, concat_axis=0, tiled=True
        ).reshape(width, rows)

    stay = [pltpu.with_memory_space_constraint(a, pltpu.HBM)
            for a in (field, forcing[0], initial, levels)]
    stay_tables = [pltpu.with_memory_space_constraint(a, pltpu.HBM) for a in tables]
    buffers = [jnp.float32, jnp.float32, jnp.int32]

    edge = call(
        edge_kernel, strip, [SMEM] + [HBM] * 4,
        scratch=[pltpu.VMEM((TILE, width), kind) for kind in [jnp.float32] + buffers]
        + [pltpu.SemaphoreType.DMA((4,))],
        flops=32 * TILE * width, bytes_accessed=24 * TILE * width,
    )(step, *stay)
    edge = lax.ppermute(edge, SLAB, [(i, (i + 1) % slabs) for i in range(slabs)])
    field, head, ready, excess, gain, *tables = call(
        functools.partial(load_kernel, steps, SHIFT),
        [plane, strip, turned, plane, gains] + [jax.ShapeDtypeStruct(t.shape, t.dtype) for t in tables],
        [SMEM] * 2 + [HBM] * (4 + len(tables)),
        scratch=[pltpu.VMEM((rows, width), kind) for kind in [jnp.float32] + buffers]
        + [pltpu.SemaphoreType.DMA((4 + len(tables),))],
        flops=work, bytes_accessed=moved_bytes,
    )(step, column, *stay, *stay_tables)
    sent = call(
        functools.partial(source_kernel, steps, SHIFT), turned, [SMEM] + [VMEM] * (4 + len(tables)),
        scratch=[pltpu.VMEM((2 * TILE, width), jnp.float32)], flops=work, bytes_accessed=moved_bytes,
    )(step, field, head, ready, edge, *tables)

    def solve(block, inverse):
        return exchange(call(
            functools.partial(solve_kernel, slabs, steps), turned, [VMEM] * (2 + 2 * len(tables)),
            flops=2 * work, bytes_accessed=moved_bytes,
        )(exchange(block), gain, *tables, *inverse))

    error, first = call(
        functools.partial(sweep_kernel, steps), [turned, plane], [SMEM] + [VMEM] * (3 + len(tables)),
        flops=2 * work, bytes_accessed=moved_bytes,
    )(step, solve(sent, shifted), field, excess, *tables)
    increment = call(
        finish_kernel, plane, [VMEM] * (2 + len(tables)), flops=work, bytes_accessed=moved_bytes
    )(solve(error, tables), first, *tables)
    return increment[None]


def solution(mesh):
    fine = jax.sharding.Mesh(mesh.devices.reshape(tuple(AXES.values())), tuple(AXES))
    placed = (P(TIME, SLAB, None), P(TIME, SLAB, None), P(SLAB, None), P(SLAB, None))
    return jax.shard_map(
        local, mesh=fine, in_specs=placed, out_specs=P(TIME, SLAB, None), check_vma=False
    )
```
